32 devices in a mesh: groups: 2 (over y), dp: 4 (over x, core), tensor: 4 (over z).
Axes of the slice: x: 2, y: 2, z: 4, core: 2. Of those that a mesh axis runs over, the one named last changes fastest.
Arguments:
- activations: bfloat16 [15360, 14336], P(('groups', 'dp'), 'tensor'), parts along dimension 0, may hold values from -6 to 6
- out_grads: bfloat16 [15360, 4096], P(('groups', 'dp'), 'tensor'), parts along dimension 0, may hold values from -6 to 6
- proj_in: bfloat16 [64, 14336], P(None, 'tensor'), may hold values from -0.046875 to 0.046875
- proj_out: bfloat16 [64, 4096], P(None, 'tensor'), may hold values from -0.09375 to 0.09375
- hess_inv: float32 [4096, 4096], P('dp', 'tensor'), may hold values from -1 to 2, as said below
- queries: bfloat16 [1536, 4096], P('dp', 'tensor'), may hold values from -6 to 6
Outputs:
- scores: float32 [120, 1536], P(('groups', 'dp'), 'tensor'), parts along dimension 0
The draws below stay inside these ranges and needn't reach their ends.
There are 2 independent parts, one for each index of `groups`. The reference program is written for one: setup_inputs(seed, part) draws one part's arguments, and reference() takes and returns one part's arrays. A program takes and returns all parts, laid end to end along the dimension named above; an argument that names none is the same for every part. Nothing has to cross between parts.
Inputs may be any that keep to these rules, and one draw needn't show every extreme that they name: hess_inv is exactly symmetric.
All inputs are finite; a program needn't handle non-finite values.
Results may differ from the reference program's by a relative error of at most 0.0003.
Values may be sent and summed in bfloat16 or wider, within the bound.
No kernel may reach another device: no remote copies, remote signals or barrier semaphores. Data moves between devices by JAX's collectives and lax.ppermute only.
A program may use at most 128 MiB of HBM per device.

```python
import math
import jax
import jax.numpy as jnp
from jax import lax

D = 4096
FF = 14336
R = 64
SEQ = 128
K = 4096
EXAMPLES = 60
TOKENS = 7680
NQ = 1536


def draw_hess_inv(key, part):
    key = jax.random.fold_in(key, 5)
    count = R * R
    base = jnp.clip(jax.random.normal(key, (count, count), jnp.float32), -4.0, 4.0)
    off_part = (base + base.T) * (0.35 / math.sqrt(2.0 * count))
    return off_part + jnp.eye(count, dtype=jnp.float32)


def levels(rng, shape, pieces, smallest, top_value):
    loudness = 1.0
    for position, blocks in pieces:
        heights = jax.random.uniform(jax.random.fold_in(jax.random.fold_in(rng, 6), position), (blocks,), jnp.float32, smallest / len(pieces), top_value / len(pieces))
        loudness = loudness * jnp.repeat(jnp.exp(heights), shape[position] // blocks).reshape((-1,) + (1,) * (len(shape) - 1 - position))
    return loudness


def noise(key, extent, scale, most, shards=(), held_as=jnp.bfloat16):
    result = scale * jax.random.normal(key, extent, jnp.float32)
    if shards:
        result = result * levels(key, extent, shards, -0.22, 0.18)
    return jnp.clip(result, -most, most).astype(held_as)


def setup_inputs(seed: int = 0, part: int = 0) -> dict:
    keys = jax.random.split(jax.random.key(seed), 7)
    part_keys = jax.random.split(jax.random.fold_in(keys[6], part), 7)
    return {
        "activations": noise(part_keys[0], (TOKENS, FF), 1.0, 6.0, ((0, 4), (1, 4))),
        "out_grads": noise(part_keys[1], (TOKENS, D), 1.0, 6.0, ((0, 4), (1, 4))),
        "proj_in": noise(keys[2], (R, FF), FF ** -0.5, 0.046875, ((1, 4),)),
        "proj_out": noise(keys[3], (R, D), D ** -0.5, 0.09375, ((1, 4),)),
        "hess_inv": draw_hess_inv(jax.random.fold_in(keys[6], 71), part),
        "queries": noise(keys[5], (NQ, K), 1.0, 6.0, ((0, 4), (1, 4))),
    }


def reference(activations, out_grads, proj_in, proj_out, hess_inv, queries):
    left = jnp.dot(out_grads, proj_out.T, preferred_element_type=jnp.float32)
    right = jnp.dot(activations, proj_in.T, preferred_element_type=jnp.float32)
    left = left.reshape(EXAMPLES, SEQ, R)
    right = right.reshape(EXAMPLES, SEQ, R)
    grads = jnp.einsum('esa,esb->eab', left, right, precision=lax.Precision.HIGHEST)
    grads = grads.reshape(EXAMPLES, R * R) * (1.0 / math.sqrt(SEQ))
    precond = jnp.dot(grads, hess_inv, precision=lax.Precision.HIGHEST)
    scores = lax.dot_general(precond, queries.astype(jnp.float32), (((1,), (1,)), ((), ())), precision=lax.Precision.HIGHEST)
    return scores * (1.0 / math.sqrt(R * R))
```

```python
import functools
import math

import jax
import jax.numpy as jnp
from jax import lax
from jax.experimental import pallas as pl
from jax.experimental.pallas import tpu as pltpu
from jax.sharding import PartitionSpec as P

R = 64
SEQ = 128
LANES = 128
TOP = 128.0
ROWS_CONTRACT = (((1,), (1,)), ((), ()))


def params(mib):
    return pltpu.CompilerParams(vmem_limit_bytes=mib << 20)


def first_example(owner, m, examples):
    return jnp.minimum(owner * m, examples - m)


def bitrev(v, bits):
    out = 0
    for b in range(bits):
        out = out + ((v >> b) & 1) * (1 << (bits - 1 - b))
    return out


def project_kernel(steps, coded, pos, acts, outs, p_in, p_out, y_ref, acc):
    k = pl.program_id(1)
    right = lax.dot_general(acts[...], p_in[...], ROWS_CONTRACT, preferred_element_type=jnp.float32)
    left = lax.dot_general(outs[...], p_out[...], ROWS_CONTRACT, preferred_element_type=jnp.float32)
    both = jnp.concatenate([left, right], 1)

    @pl.when(k == 0)
    def _():
        acc[...] = both

    @pl.when(k > 0)
    def _():
        acc[...] += both

    @pl.when(k == steps - 1)
    def _():
        x = acc[...]
        if not coded:
            y_ref[0] = x
        else:
            rows = x.shape[0]
            top = jnp.maximum(jnp.max(jnp.abs(x), axis=0, keepdims=True), 1e-30)
            top = top.astype(jnp.bfloat16).astype(jnp.float32)
            w = x * (TOP / top)
            s = w * w
            s = s * s
            s = s * s
            s = s * s
            y = jnp.where(x < 0, -s, s)
            y_ref[0, pl.ds(0, rows), :] = y.astype(jnp.bfloat16)
            y_ref[0, pl.ds(rows, 16), :] = jnp.broadcast_to(top, (16, LANES)).astype(jnp.bfloat16)


def project(pos, acts, outs, p_in, p_out, shifts, coded, n, m):
    examples = acts.shape[0] // SEQ
    rows = m * SEQ
    steps = 1
    for c in (8, 4, 2):
        if acts.shape[1] % (c * LANES) == 0 and outs.shape[1] % (c * LANES) == 0:
            steps = c
            break
    wide_in, wide_out = acts.shape[1] // steps, outs.shape[1] // steps
    first, stride = shifts[0], (shifts[1] - shifts[0] if len(shifts) > 1 else 0)

    def start(i, pos):
        owner = lax.rem(pos[1] + first + stride * i, n)
        return first_example(owner, m, examples) * SEQ

    out_rows = rows + 16 if coded else rows
    dtype = jnp.bfloat16 if coded else jnp.float32
    count = len(shifts)
    return pl.pallas_call(
        functools.partial(project_kernel, steps, coded),
        grid_spec=pltpu.PrefetchScalarGridSpec(
            num_scalar_prefetch=1,
            grid=(count, steps),
            in_specs=[
                pl.BlockSpec((pl.Element(rows), pl.Element(wide_in)), lambda i, k, pos: (start(i, pos), k * wide_in)),
                pl.BlockSpec((pl.Element(rows), pl.Element(wide_out)), lambda i, k, pos: (start(i, pos), k * wide_out)),
                pl.BlockSpec((R, wide_in), lambda i, k, pos: (0, k)),
                pl.BlockSpec((R, wide_out), lambda i, k, pos: (0, k)),
            ],
            out_specs=pl.BlockSpec((1, out_rows, LANES), lambda i, k, pos: (i, 0, 0)),
            scratch_shapes=[pltpu.VMEM((rows, LANES), jnp.float32)],
        ),
        out_shape=jax.ShapeDtypeStruct((count, out_rows, LANES), dtype),
        compiler_params=params(24),
        cost_estimate=pl.CostEstimate(
            flops=8 * count * rows * (acts.shape[1] + outs.shape[1]) * R,
            bytes_accessed=2 * count * rows * (acts.shape[1] + outs.shape[1]),
            transcendentals=0,
        ),
    )(pos, acts, outs, p_in, p_out)


def grads_kernel(n, m, bits, pos, own, *refs):
    coded, out, z = refs[: n - 1], refs[n - 1], refs[n]
    rows = m * SEQ
    x = own[...]
    for ref in coded:
        y = ref[pl.ds(0, rows), :].astype(jnp.float32)
        top = ref[pl.ds(rows, 1), :].astype(jnp.float32) * (1.0 / TOP)
        w = jnp.sqrt(jnp.sqrt(jnp.sqrt(jnp.sqrt(jnp.abs(y)))))
        x = x + jnp.where(y < 0, -w, w) * top
    half = R // n // 2
    d = pos[0]
    for e in range(m):
        xe = x[e * SEQ : (e + 1) * SEQ, :]
        z[...] = lax.dot_general(
            xe.T, xe, (((1,), (0,)), ((), ())), precision=lax.Precision.HIGHEST, preferred_element_type=jnp.float32
        )
        for j in range(n):
            at = bitrev(lax.bitwise_xor(d, j), bits)
            even = z[pl.ds(2 * half * j, half, stride=2), :]
            odd = z[pl.ds(2 * half * j + 1, half, stride=2), :]
            out[at, :, e, :] = jnp.concatenate([even[:, R:], odd[:, R:]], 1)


def grads_of(pos, own, coded, n, m, bits):
    half = R // n // 2
    return pl.pallas_call(
        functools.partial(grads_kernel, n, m, bits),
        in_specs=[pl.BlockSpec(memory_space=pltpu.SMEM)] + [pl.BlockSpec(memory_space=pltpu.VMEM)] * n,
        out_specs=pl.BlockSpec(memory_space=pltpu.VMEM),
        out_shape=jax.ShapeDtypeStruct((n, half, m, LANES), jnp.float32),
        scratch_shapes=[pltpu.VMEM((SEQ, LANES), jnp.float32)],
        compiler_params=params(24),
    )(pos, own, *coded)


def split(v):
    hi = v.astype(jnp.bfloat16)
    return hi, (v - hi.astype(jnp.float32)).astype(jnp.bfloat16)


def scores_kernel(n, m, bits, pos, h_hi, h_lo, queries, *refs):
    grads, out, a = refs[:n], refs[n], refs[n + 1]
    half = grads[0].shape[0]
    group = n * m
    rows = n * group
    for p in range(n):
        for r in range(half):
            a[pl.ds(p * group, group), pl.ds(r * LANES, LANES)] = grads[p][r]
    contract = (((1,), (0,)), ((), ()))
    hi, lo = split(a[...])
    top = lax.dot_general(jnp.concatenate([hi, lo], 0), h_hi[...], contract, preferred_element_type=jnp.float32)
    low = lax.dot_general(hi, h_lo[...], contract, preferred_element_type=jnp.float32)
    hi, lo = split(top[:rows] + top[rows:] + low)
    both = jnp.concatenate([hi, lo], 0)
    d, t = pos[0], pos[1]

    def one(u):
        block = bitrev(lax.bitwise_xor(d, lax.rem(t + u, n)), bits)
        s = lax.dot_general(both, queries[block], ROWS_CONTRACT, preferred_element_type=jnp.float32)
        s = s[:rows] + s[rows:]
        for p in range(n):
            owner = lax.rem(t - p + n, n)
            for b in range(n):
                at = p * group + b * m
                out[b, u, owner] = s[at : at + m]

    if n <= 4:
        for u in range(n):
            one(u)
    else:
        lax.fori_loop(0, n, lambda u, c: (one(u), c)[1], 0)


def scores_of(pos, h_hi, h_lo, queries, grads, n, m, bits):
    half, group, _ = grads[0].shape
    width = queries.shape[1]
    rows = n * group
    return pl.pallas_call(
        functools.partial(scores_kernel, n, m, bits),
        in_specs=[pl.BlockSpec(memory_space=pltpu.SMEM)] + [pl.BlockSpec(memory_space=pltpu.VMEM)] * (3 + n),
        out_specs=pl.BlockSpec(memory_space=pltpu.VMEM),
        out_shape=jax.ShapeDtypeStruct((n, n, n, m, width), jnp.float32),
        scratch_shapes=[pltpu.VMEM((rows, half * LANES), jnp.float32)],
        compiler_params=params(40),
    )(pos, h_hi, h_lo, queries, *grads)


def local(n, activations, out_grads, proj_in, proj_out, hess_inv, queries):
    bits = n.bit_length() - 1
    examples = activations.shape[0] // SEQ
    m = -(-examples // n)
    pos = jnp.stack([lax.axis_index("dp"), lax.axis_index("tensor")]).astype(jnp.int32)

    def shift(v, s):
        return lax.ppermute(v, "tensor", [(i, (i + s) % n) for i in range(n)])

    def flip(v, mask):
        return lax.ppermute(v, "dp", [(i, i ^ mask) for i in range(n)])

    all_q = queries[None]
    for b in reversed(range(bits)):
        all_q = jnp.concatenate([all_q, flip(all_q, 1 << b)], 0)

    order = sorted(range(1, n), key=lambda s: -min(s, n - s))
    sent = {}
    for s in order:
        y = project(pos, activations, out_grads, proj_in, proj_out, (s,), True, n, m)
        sent[s] = shift(y[0], s)
    own = project(pos, activations, out_grads, proj_in, proj_out, (0,), False, n, m)[0]

    h_top = lax.reduce_precision(hess_inv, 8, 7)
    h_hi = h_top.astype(jnp.bfloat16)
    h_lo = (hess_inv - h_top).astype(jnp.bfloat16)

    grads = grads_of(pos, own, [sent[s] for s in order], n, m, bits)
    parts = [grads[0]] + [flip(grads[p], bitrev(p, bits)) for p in range(1, n)]
    group = jnp.concatenate(parts, 1)
    groups = [group] + [shift(group, s) for s in range(1, n)]

    out = scores_of(pos, h_hi, h_lo, all_q, groups, n, m, bits)
    for b in range(bits):
        half = out.shape[0] // 2
        out = out[:half] + flip(out[half:], 1 << b)
    out = out[0]
    total = out[0]
    for s in range(1, n):
        total = total + shift(out[s], s)
    width = total.shape[-1]
    total = total.reshape(n * m, width)
    rows, i = [], 0
    while i < examples:
        owner = min(i // m, n - 1)
        begin = min(owner * m, examples - m)
        stop = begin + m
        rows.append(total[owner * m + i - begin : owner * m + stop - begin])
        i = stop
    scale = (1.0 / math.sqrt(SEQ)) * (1.0 / math.sqrt(R * R))
    return jnp.concatenate(rows, 0)[:examples] * scale


def solution(mesh):
    n = mesh.shape["tensor"]
    return jax.shard_map(
        functools.partial(local, n),
        mesh=mesh,
        in_specs=(
            P(("groups", "dp"), "tensor"),
            P(("groups", "dp"), "tensor"),
            P(None, "tensor"),
            P(None, "tensor"),
            P("dp", "tensor"),
            P("dp", "tensor"),
        ),
        out_specs=P(("groups", "dp"), "tensor"),
        check_vma=False,
    )
```

```python
import functools
import math

import jax
import jax.numpy as jnp
from jax import lax
from jax.experimental import pallas as pl
from jax.experimental.pallas import tpu as pltpu
from jax.sharding import PartitionSpec as P

R = 64
SEQ = 128
LANES = 128
TOP = 128.0
ROWS_CONTRACT = (((1,), (1,)), ((), ()))


def params(mib):
    return pltpu.CompilerParams(vmem_limit_bytes=mib << 20)


def first_example(owner, m, examples):
    return jnp.minimum(owner * m, examples - m)


def bitrev(v, bits):
    out = 0
    for b in range(bits):
        out = out + ((v >> b) & 1) * (1 << (bits - 1 - b))
    return out


def encode(x, y_ref):
    rows = x.shape[0]
    top = jnp.maximum(jnp.max(jnp.abs(x), axis=0, keepdims=True), 1e-30)
    top = top.astype(jnp.bfloat16).astype(jnp.float32)
    w = x * (TOP / top)
    s = w * w
    s = s * s
    s = s * s
    s = s * s
    y = jnp.where(x < 0, -s, s)
    y_ref[pl.ds(0, rows), :] = y.astype(jnp.bfloat16)
    y_ref[pl.ds(rows, 16), :] = jnp.broadcast_to(top, (16, LANES)).astype(jnp.bfloat16)


def project_kernel(masks, acts, outs, p_in, p_out, *refs):
    y_refs, acc = refs[:-1], refs[-1]
    right = lax.dot_general(acts[...], p_in[...], ROWS_CONTRACT, preferred_element_type=jnp.float32)
    left = lax.dot_general(outs[...], p_out[...], ROWS_CONTRACT, preferred_element_type=jnp.float32)
    acc[...] = jnp.concatenate([left, right], 1)

    def finish(mask, y_ref):
        if mask == 0:
            y_ref[...] = acc[...]
        else:
            encode(acc[...], y_ref)

    for i, (mask, y_ref) in enumerate(zip(masks, y_refs)):
        pl.when(pl.program_id(0) == i)(functools.partial(finish, mask, y_ref))


def project(acts, outs, p_in, p_out, masks, m):
    examples = acts.shape[0] // SEQ
    rows = m * SEQ
    first = masks[0]

    def start(i):
        return first_example(lax.bitwise_xor(lax.axis_index("tensor"), first - i), m, examples) * SEQ

    shapes = [
        jax.ShapeDtypeStruct((rows + 16, LANES), jnp.bfloat16) if k else jax.ShapeDtypeStruct((rows, LANES), jnp.float32)
        for k in masks
    ]
    return pl.pallas_call(
        functools.partial(project_kernel, masks),
        grid=(len(masks),),
        in_specs=[
            pl.BlockSpec((pl.Element(rows), pl.Element(acts.shape[1])), lambda i: (start(i), 0)),
            pl.BlockSpec((pl.Element(rows), pl.Element(outs.shape[1])), lambda i: (start(i), 0)),
            pl.BlockSpec(p_in.shape, lambda i: (0, 0)),
            pl.BlockSpec(p_out.shape, lambda i: (0, 0)),
        ],
        out_specs=[pl.BlockSpec(s.shape, lambda i: (0, 0)) for s in shapes],
        scratch_shapes=[pltpu.VMEM((rows, LANES), jnp.float32)],
        out_shape=shapes,
        compiler_params=params(59),
        cost_estimate=pl.CostEstimate(flops=1, bytes_accessed=1, transcendentals=0),
    )(acts, outs, p_in, p_out)


def split(v):
    hi = v.astype(jnp.bfloat16)
    return hi, (v - hi.astype(jnp.float32)).astype(jnp.bfloat16)


def grads_kernel(n, m, bits, own, *refs):
    coded, out, z = refs[: n - 1], refs[n - 1], refs[n]
    rows = m * SEQ
    x = own[...]
    for ref in coded:
        y = ref[pl.ds(0, rows), :].astype(jnp.float32)
        top = ref[pl.ds(rows, 16), :].astype(jnp.float32)[:1] * (1.0 / TOP)
        w = lax.rsqrt(lax.rsqrt(lax.rsqrt(lax.rsqrt(jnp.abs(y)))))
        x = x + jnp.where(y < 0, -w, w) * top
    half = R // n // 2
    d = lax.axis_index("dp")
    contract = (((1,), (0,)), ((), ()))
    for e in range(m):
        xe = x[e * SEQ : (e + 1) * SEQ, :]
        hi, lo = split(xe)
        hi_t, lo_t = split(xe.T)
        first = lax.dot_general(jnp.concatenate([hi_t, lo_t], 0), hi, contract, preferred_element_type=jnp.float32)
        last = lax.dot_general(hi_t, lo, contract, preferred_element_type=jnp.float32)
        z[e] = first[:LANES] + first[LANES:] + last
    for e in range(m):
        for j in range(n):
            at = bitrev(lax.bitwise_xor(d, j), bits)
            even = z[e, pl.ds(2 * half * j, half, stride=2), :]
            odd = z[e, pl.ds(2 * half * j + 1, half, stride=2), :]
            out[at, :, e, :] = jnp.concatenate([even[:, R:], odd[:, R:]], 1)


def grads_of(own, coded, n, m, bits):
    half = R // n // 2
    return pl.pallas_call(
        functools.partial(grads_kernel, n, m, bits),
        in_specs=[pl.BlockSpec(memory_space=pltpu.VMEM)] * n,
        out_specs=pl.BlockSpec(memory_space=pltpu.VMEM),
        out_shape=jax.ShapeDtypeStruct((n, half, m, LANES), jnp.float32),
        scratch_shapes=[pltpu.VMEM((m, SEQ, LANES), jnp.float32)],
        compiler_params=params(24),
    )(own, *coded)


def scores_kernel(n, m, masks, h_hi, h_lo, *refs):
    queries, grads, out, a = refs[:n], refs[n : 2 * n], refs[2 * n], refs[2 * n + 1]
    half = grads[0].shape[0]
    group = n * m
    rows = n * group
    for p in range(n):
        for r in range(half):
            a[pl.ds(p * group, group), pl.ds(r * LANES, LANES)] = grads[p][r]
    contract = (((1,), (0,)), ((), ()))
    hi, lo = split(a[...])
    top = lax.dot_general(jnp.concatenate([hi, lo], 0), h_hi[...], contract, preferred_element_type=jnp.float32)
    low = lax.dot_general(hi, h_lo[...], contract, preferred_element_type=jnp.float32)
    hi, lo = split(top[:rows] + top[rows:] + low)
    both = jnp.concatenate([hi, lo], 0)
    d, t = lax.axis_index("dp"), lax.axis_index("tensor")
    for mask, ref in zip(masks, queries):
        to = lax.bitwise_xor(lax.bitwise_xor(d, mask), t)
        s = lax.dot_general(both, ref[...], ROWS_CONTRACT, preferred_element_type=jnp.float32)
        s = s[:rows] + s[rows:]
        for p in range(n):
            for b in range(n):
                at = p * group + b * m
                out[b, to, lax.bitwise_xor(t, p)] = s[at : at + m]


def scores_of(h_hi, h_lo, queries, grads, n, m):
    half, group, _ = grads[0].shape
    masks = sorted(queries)
    blocks = [queries[k] for k in masks]
    width = blocks[0].shape[0]
    rows = n * group
    return pl.pallas_call(
        functools.partial(scores_kernel, n, m, masks),
        in_specs=[pl.BlockSpec(memory_space=pltpu.VMEM)] * (2 + 2 * n),
        out_specs=pl.BlockSpec(memory_space=pltpu.VMEM),
        out_shape=jax.ShapeDtypeStruct((n, n, n, m, width), jnp.float32),
        scratch_shapes=[pltpu.VMEM((rows, half * LANES), jnp.float32)],
        compiler_params=params(40),
    )(h_hi, h_lo, *blocks, *grads)


def local(n, activations, out_grads, proj_in, proj_out, hess_inv, queries):
    bits = n.bit_length() - 1
    examples = activations.shape[0] // SEQ
    m = -(-examples // n)
    def along(v, mask):
        return lax.ppermute(v, "tensor", [(i, i ^ mask) for i in range(n)])

    def flip(v, mask):
        return lax.ppermute(v, "dp", [(i, i ^ mask) for i in range(n)])

    def after(v, first):
        return lax.optimization_barrier((v, first))[0]

    all_q = {0: queries}
    all_q[n // 2] = flip(queries, n // 2)

    far = list(range(n - 1, 1, -1))
    y = project(activations, out_grads, proj_in, proj_out, far, m)
    near, own = project(activations, after(out_grads, y), proj_in, proj_out, [1, 0], m)
    coded = [along(v, mask) for v, mask in zip(y, far)] + [along(near, 1)]

    own, all_q[n // 2] = lax.optimization_barrier((own, all_q[n // 2]))
    grads = grads_of(own, coded, n, m, bits)
    parts = [flip(grads[p], bitrev(p, bits)) for p in range(1, n)]
    hess_inv = after(hess_inv, grads)
    h_top = lax.reduce_precision(hess_inv, 8, 7)
    h_hi = h_top.astype(jnp.bfloat16)
    h_lo = (hess_inv - h_top).astype(jnp.bfloat16)
    first, h_hi, h_lo = lax.optimization_barrier((grads[0], h_hi, h_lo))
    parts = [first] + parts
    group = jnp.concatenate(parts, 1)
    groups = [group] + [along(group, s) for s in range(1, n)]

    for b in reversed(range(bits - 1)):
        keys = list(all_q)
        all_q = dict(zip(keys, after(tuple(all_q.values()), group)))
        all_q.update({k | (1 << b): flip(v, 1 << b) for k, v in all_q.items()})

    out = scores_of(h_hi, h_lo, all_q, groups, n, m)
    for b in range(bits):
        half = out.shape[0] // 2
        out = out[:half] + flip(out[half:], 1 << b)
    out = out[0]
    total = out[0]
    for s in range(1, n):
        total = total + along(out[s], s)
    width = total.shape[-1]
    total = total.reshape(n * m, width)
    rows, i = [], 0
    while i < examples:
        owner = min(i // m, n - 1)
        begin = min(owner * m, examples - m)
        stop = begin + m
        rows.append(total[owner * m + i - begin : owner * m + stop - begin])
        i = stop
    scale = (1.0 / math.sqrt(SEQ)) * (1.0 / math.sqrt(R * R))
    return jnp.concatenate(rows, 0)[:examples] * scale


def solution(mesh):
    n = mesh.shape["tensor"]
    return jax.shard_map(
        functools.partial(local, n),
        mesh=mesh,
        in_specs=(
            P(("groups", "dp"), "tensor"),
            P(("groups", "dp"), "tensor"),
            P(None, "tensor"),
            P(None, "tensor"),
            P("dp", "tensor"),
            P("dp", "tensor"),
        ),
        out_specs=P(("groups", "dp"), "tensor"),
        check_vma=False,
    )
```

```python
import functools
import math

import jax
import jax.numpy as jnp
from jax import lax
from jax.experimental import pallas as pl
from jax.experimental.pallas import tpu as pltpu
from jax.sharding import PartitionSpec as P

R = 64
SEQ = 128
LANES = 128
TOP = 128.0
ROWS_CONTRACT = (((1,), (1,)), ((), ()))


def params(mib):
    return pltpu.CompilerParams(vmem_limit_bytes=mib << 20)


def first_example(owner, m, examples):
    return jnp.minimum(owner * m, examples - m)


def bitrev(v, bits):
    out = 0
    for b in range(bits):
        out = out + ((v >> b) & 1) * (1 << (bits - 1 - b))
    return out


def power(x, top):
    w = x * (TOP / top)
    s = w * w
    s = s * s
    s = s * s
    s = s * s
    return jnp.where(x < 0, -s, s)


def root(y):
    w = lax.rsqrt(lax.rsqrt(lax.rsqrt(lax.rsqrt(jnp.abs(y)))))
    return jnp.where(y < 0, -w, w)


def column_top(x):
    top = jnp.maximum(jnp.max(jnp.abs(x), axis=0, keepdims=True), 1e-30)
    return top.astype(jnp.bfloat16).astype(jnp.float32)


def encode(x, y_ref):
    rows = x.shape[0]
    top = column_top(x)
    y_ref[pl.ds(0, rows), :] = power(x, top).astype(jnp.bfloat16)
    y_ref[pl.ds(rows, 16), :] = jnp.broadcast_to(top, (16, LANES)).astype(jnp.bfloat16)


def project_kernel(masks, acts, outs, p_in, p_out, *refs):
    y_refs, acc = refs[:-1], refs[-1]
    right = lax.dot_general(acts[...], p_in[...], ROWS_CONTRACT, preferred_element_type=jnp.float32)
    left = lax.dot_general(outs[...], p_out[...], ROWS_CONTRACT, preferred_element_type=jnp.float32)
    acc[...] = jnp.concatenate([left, right], 1)

    def finish(mask, y_ref):
        if mask == 0:
            y_ref[...] = acc[...]
        else:
            encode(acc[...], y_ref)

    for i, (mask, y_ref) in enumerate(zip(masks, y_refs)):
        pl.when(pl.program_id(0) == i)(functools.partial(finish, mask, y_ref))


def project(acts, outs, p_in, p_out, masks, m, mib):
    examples = acts.shape[0] // SEQ
    rows = m * SEQ
    first = masks[0]

    def start(i):
        return first_example(lax.bitwise_xor(lax.axis_index("tensor"), first - i), m, examples) * SEQ

    shapes = [
        jax.ShapeDtypeStruct((rows + 16, LANES), jnp.bfloat16) if k else jax.ShapeDtypeStruct((rows, LANES), jnp.float32)
        for k in masks
    ]
    return pl.pallas_call(
        functools.partial(project_kernel, masks),
        grid=(len(masks),),
        in_specs=[
            pl.BlockSpec((pl.Element(rows), pl.Element(acts.shape[1])), lambda i: (start(i), 0)),
            pl.BlockSpec((pl.Element(rows), pl.Element(outs.shape[1])), lambda i: (start(i), 0)),
            pl.BlockSpec(p_in.shape, lambda i: (0, 0)),
            pl.BlockSpec(p_out.shape, lambda i: (0, 0)),
        ],
        out_specs=[pl.BlockSpec(s.shape, lambda i: (0, 0)) for s in shapes],
        scratch_shapes=[pltpu.VMEM((rows, LANES), jnp.float32)],
        out_shape=shapes,
        compiler_params=params(mib),
        cost_estimate=pl.CostEstimate(flops=1, bytes_accessed=1, transcendentals=0),
    )(acts, outs, p_in, p_out)


def split(v):
    hi = v.astype(jnp.bfloat16)
    return hi, (v - hi.astype(jnp.float32)).astype(jnp.bfloat16)


def grads_kernel(n, m, bits, own, *refs):
    coded, out, z, block = refs[: n - 1], *refs[-3:]
    rows = m * SEQ
    x = own[...]
    for ref in coded:
        y = ref[...].astype(jnp.float32)
        x = x + root(y[:rows]) * y[rows : rows + 1]
    half = R // n // 2
    d = lax.axis_index("dp")
    contract = (((1,), (0,)), ((), ()))
    for e in range(m):
        xe = x[e * SEQ : (e + 1) * SEQ, :]
        hi, lo = split(xe)
        hi_t, lo_t = split(xe.T)
        first = lax.dot_general(jnp.concatenate([hi_t, lo_t], 0), hi, contract, preferred_element_type=jnp.float32)
        last = lax.dot_general(hi_t, lo, contract, preferred_element_type=jnp.float32)
        z[e] = first[:LANES] + first[LANES:] + last
    for j in range(n):
        for e in range(m):
            even = z[e, pl.ds(2 * half * j, half, stride=2), :]
            odd = z[e, pl.ds(2 * half * j + 1, half, stride=2), :]
            g = jnp.concatenate([even[:, R:], odd[:, R:]], 1)
            top = column_top(g)
            block[pl.ds(e, half, stride=m), :] = power(g, top)
            block[pl.ds(half * m + e, 1), :] = top
        out[bitrev(lax.bitwise_xor(d, j), bits)] = block[...].astype(jnp.bfloat16)


def grads_of(own, coded, n, m, bits):
    rows = (R // n // 2 + 1) * m
    return pl.pallas_call(
        functools.partial(grads_kernel, n, m, bits),
        in_specs=[pl.BlockSpec(memory_space=pltpu.VMEM)] * n,
        out_specs=pl.BlockSpec(memory_space=pltpu.VMEM),
        out_shape=jax.ShapeDtypeStruct((n, rows, LANES), jnp.bfloat16),
        scratch_shapes=[pltpu.VMEM((m, SEQ, LANES), jnp.float32), pltpu.VMEM((rows, LANES), jnp.float32)],
        compiler_params=params(24),
        cost_estimate=pl.CostEstimate(flops=1, bytes_accessed=1, transcendentals=0),
    )(own, *coded)


def halves_kernel(h, *refs):
    hi, lo = split(h[...])
    refs[-2][...] = hi
    refs[-1][...] = lo


def halves(h, wait_for):
    rows = h.shape[0] // 4 if h.shape[0] % 64 == 0 else h.shape[0]
    spec = pl.BlockSpec((rows, h.shape[1]), lambda i: (i, 0))
    shape = jax.ShapeDtypeStruct(h.shape, jnp.bfloat16)
    return pl.pallas_call(
        halves_kernel,
        grid=(h.shape[0] // rows,),
        in_specs=[spec] + [pl.BlockSpec(memory_space=pl.ANY)] * len(wait_for),
        out_specs=[spec, spec],
        out_shape=[shape, shape],
        compiler_params=params(24),
        cost_estimate=pl.CostEstimate(flops=1, bytes_accessed=1, transcendentals=0),
    )(h, *wait_for)


def scores_kernel(n, m, masks, h_hi, h_lo, *refs):
    queries, grads, out, a = refs[:n], refs[n : 2 * n], refs[2 * n], refs[2 * n + 1]
    half = R // n // 2
    rows = n * n * m
    for s in range(n * n):
        y = grads[s // n][s % n].astype(jnp.float32)
        top = y[half * m :]
        w = root(y[: half * m]) * (1.0 / TOP)
        for r in range(half):
            a[pl.ds(s * m, m), pl.ds(r * LANES, LANES)] = w[r * m : (r + 1) * m] * top
    contract = (((1,), (0,)), ((), ()))
    hi, lo = split(a[...])
    top = lax.dot_general(jnp.concatenate([hi, lo], 0), h_hi[...], contract, preferred_element_type=jnp.float32)
    low = lax.dot_general(hi, h_lo[...], contract, preferred_element_type=jnp.float32)
    hi, lo = split(top[:rows] + top[rows:] + low)
    both = jnp.concatenate([hi, lo], 0)
    d, t = lax.axis_index("dp"), lax.axis_index("tensor")
    for mask, ref in zip(masks, queries):
        to = lax.bitwise_xor(lax.bitwise_xor(d, mask), t)
        s = lax.dot_general(both, ref[...], ROWS_CONTRACT, preferred_element_type=jnp.float32)
        s = s[:rows] + s[rows:]
        for p in range(n):
            for b in range(n):
                at = (p * n + b) * m
                out[b, to, lax.bitwise_xor(t, p)] = s[at : at + m]


def scores_of(h_hi, h_lo, queries, grads, n, m):
    masks = sorted(queries)
    blocks = [queries[k] for k in masks]
    width = blocks[0].shape[0]
    return pl.pallas_call(
        functools.partial(scores_kernel, n, m, masks),
        in_specs=[pl.BlockSpec(memory_space=pltpu.VMEM)] * (2 + 2 * n),
        out_specs=pl.BlockSpec(memory_space=pltpu.VMEM),
        out_shape=jax.ShapeDtypeStruct((n, n, n, m, width), jnp.float32),
        scratch_shapes=[pltpu.VMEM((n * n * m, R // n // 2 * LANES), jnp.float32)],
        compiler_params=params(40),
    )(h_hi, h_lo, *blocks, *grads)


def local(n, activations, out_grads, proj_in, proj_out, hess_inv, queries):
    bits = n.bit_length() - 1
    examples = activations.shape[0] // SEQ
    m = -(-examples // n)
    def along(v, mask):
        return lax.ppermute(v, "tensor", [(i, i ^ mask) for i in range(n)])

    def flip(v, mask):
        return lax.ppermute(v, "dp", [(i, i ^ mask) for i in range(n)])

    def after(v, first):
        return lax.optimization_barrier((v, first))[0]

    all_q = {0: queries}
    all_q[n // 2] = flip(queries, n // 2)

    far = list(range(n - 1, 1, -1))
    y = project(activations, out_grads, proj_in, proj_out, far, m, 59)
    near, own = project(activations, after(out_grads, y), proj_in, proj_out, [1, 0], m, 58)
    coded = [along(v, mask) for v, mask in zip(y, far)] + [along(near, 1)]
    grads = grads_of(own * TOP, coded, n, m, bits)
    h_hi, h_lo = halves(hess_inv, [grads, all_q[n // 2]])
    parts = [flip(grads[p], bitrev(p, bits)) for p in range(1, n)]
    first, h_hi, h_lo = lax.optimization_barrier((grads[0], h_hi, h_lo))
    group = jnp.stack([first] + parts)
    groups = [group] + [along(group, s) for s in range(1, n)]
    for b in reversed(range(bits - 1)):
        all_q = dict(zip(all_q, after(tuple(all_q.values()), group)))
        all_q.update({k | (1 << b): flip(v, 1 << b) for k, v in all_q.items()})

    out = scores_of(h_hi, h_lo, all_q, groups, n, m)
    for b in range(bits):
        half = out.shape[0] // 2
        out = out[:half] + flip(out[half:], 1 << b)
    out = out[0]
    total = out[0]
    for s in range(1, n):
        total = total + along(out[s], s)
    width = total.shape[-1]
    total = total.reshape(n * m, width)
    rows, i = [], 0
    while i < examples:
        owner = min(i // m, n - 1)
        begin = min(owner * m, examples - m)
        stop = begin + m
        rows.append(total[owner * m + i - begin : owner * m + stop - begin])
        i = stop
    scale = (1.0 / math.sqrt(SEQ)) * (1.0 / math.sqrt(R * R)) / (TOP * TOP)
    return jnp.concatenate(rows, 0)[:examples] * scale


def solution(mesh):
    n = mesh.shape["tensor"]
    return jax.shard_map(
        functools.partial(local, n),
        mesh=mesh,
        in_specs=(
            P(("groups", "dp"), "tensor"),
            P(("groups", "dp"), "tensor"),
            P(None, "tensor"),
            P(None, "tensor"),
            P("dp", "tensor"),
            P("dp", "tensor"),
        ),
        out_specs=P(("groups", "dp"), "tensor"),
        check_vma=False,
    )
```

```python
import functools
import math

import jax
import jax.numpy as jnp
from jax import lax
from jax.experimental import pallas as pl
from jax.experimental.pallas import tpu as pltpu
from jax.sharding import PartitionSpec as P

R = 64
SEQ = 128
LANES = 128
TOP = 128.0
ROWS_CONTRACT = (((1,), (1,)), ((), ()))


def params(mib):
    return pltpu.CompilerParams(vmem_limit_bytes=mib << 20)


def first_example(owner, m, examples):
    return jnp.minimum(owner * m, examples - m)


def bitrev(v, bits):
    out = 0
    for b in range(bits):
        out = out + ((v >> b) & 1) * (1 << (bits - 1 - b))
    return out


def power(x, top):
    w = x * (TOP / top)
    s = w * w
    s = s * s
    s = s * s
    s = s * s
    return jnp.where(x < 0, -s, s)


def root(y):
    w = lax.rsqrt(lax.rsqrt(lax.rsqrt(lax.rsqrt(jnp.abs(y)))))
    return jnp.where(y < 0, -w, w)


def column_top(x):
    top = jnp.maximum(jnp.max(jnp.abs(x), axis=0, keepdims=True), 1e-30)
    return top.astype(jnp.bfloat16).astype(jnp.float32)


def encode(x, y_ref):
    rows = x.shape[0]
    top = column_top(x)
    y_ref[pl.ds(0, rows), :] = power(x, top).astype(jnp.bfloat16)
    y_ref[pl.ds(rows, 16), :] = jnp.broadcast_to(top, (16, LANES)).astype(jnp.bfloat16)


def project_kernel(masks, acts, outs, p_in, p_out, *refs):
    y_refs, acc = refs[:-1], refs[-1]
    right = lax.dot_general(acts[...], p_in[...], ROWS_CONTRACT, preferred_element_type=jnp.float32)
    left = lax.dot_general(outs[...], p_out[...], ROWS_CONTRACT, preferred_element_type=jnp.float32)
    acc[...] = jnp.concatenate([left, right], 1)

    def finish(mask, y_ref):
        if mask == 0:
            y_ref[...] = acc[...]
        else:
            encode(acc[...], y_ref)

    for i, (mask, y_ref) in enumerate(zip(masks, y_refs)):
        pl.when(pl.program_id(0) == i)(functools.partial(finish, mask, y_ref))


def project(acts, outs, p_in, p_out, masks, m, mib):
    examples = acts.shape[0] // SEQ
    rows = m * SEQ
    first = masks[0]

    def start(i):
        return first_example(lax.bitwise_xor(lax.axis_index("tensor"), first - i), m, examples) * SEQ

    shapes = [
        jax.ShapeDtypeStruct((rows + 16, LANES), jnp.bfloat16) if k else jax.ShapeDtypeStruct((rows, LANES), jnp.float32)
        for k in masks
    ]
    return pl.pallas_call(
        functools.partial(project_kernel, masks),
        grid=(len(masks),),
        in_specs=[
            pl.BlockSpec((pl.Element(rows), pl.Element(acts.shape[1])), lambda i: (start(i), 0)),
            pl.BlockSpec((pl.Element(rows), pl.Element(outs.shape[1])), lambda i: (start(i), 0)),
            pl.BlockSpec(p_in.shape, lambda i: (0, 0)),
            pl.BlockSpec(p_out.shape, lambda i: (0, 0)),
        ],
        out_specs=[pl.BlockSpec(s.shape, lambda i: (0, 0)) for s in shapes],
        scratch_shapes=[pltpu.VMEM((rows, LANES), jnp.float32)],
        out_shape=shapes,
        compiler_params=params(mib),
        cost_estimate=pl.CostEstimate(flops=1, bytes_accessed=1, transcendentals=0),
    )(acts, outs, p_in, p_out)


def split(v):
    hi = v.astype(jnp.bfloat16)
    return hi, (v - hi.astype(jnp.float32)).astype(jnp.bfloat16)


def grads_kernel(n, m, bits, own, *refs):
    coded, out, z, block = refs[: n - 1], *refs[-3:]
    rows = m * SEQ
    x = own[...]
    for ref in coded:
        y = ref[...].astype(jnp.float32)
        x = x + root(y[:rows]) * y[rows : rows + 1]
    half = R // n // 2
    d = lax.axis_index("dp")
    contract = (((1,), (0,)), ((), ()))
    for e in range(m):
        xe = x[e * SEQ : (e + 1) * SEQ, :]
        hi, lo = split(xe)
        hi_t, lo_t = split(xe.T)
        first = lax.dot_general(jnp.concatenate([hi_t, lo_t], 0), hi, contract, preferred_element_type=jnp.float32)
        last = lax.dot_general(hi_t, lo, contract, preferred_element_type=jnp.float32)
        z[e] = first[:LANES] + first[LANES:] + last
    for j in range(n):
        for e in range(m):
            even = z[e, pl.ds(2 * half * j, half, stride=2), :]
            odd = z[e, pl.ds(2 * half * j + 1, half, stride=2), :]
            g = jnp.concatenate([even[:, R:], odd[:, R:]], 1)
            top = column_top(g)
            block[pl.ds(e, half, stride=m), :] = power(g, top)
            block[pl.ds(half * m + e, 1), :] = top
        out[bitrev(lax.bitwise_xor(d, j), bits)] = block[...].astype(jnp.bfloat16)


def grads_of(own, coded, n, m, bits):
    rows = (R // n // 2 + 1) * m
    return pl.pallas_call(
        functools.partial(grads_kernel, n, m, bits),
        in_specs=[pl.BlockSpec(memory_space=pltpu.VMEM)] * n,
        out_specs=pl.BlockSpec(memory_space=pltpu.VMEM),
        out_shape=jax.ShapeDtypeStruct((n, rows, LANES), jnp.bfloat16),
        scratch_shapes=[pltpu.VMEM((m, SEQ, LANES), jnp.float32), pltpu.VMEM((rows, LANES), jnp.float32)],
        compiler_params=params(24),
        cost_estimate=pl.CostEstimate(flops=1, bytes_accessed=1, transcendentals=0),
    )(own, *coded)


def halves_kernel(h, *refs):
    hi, lo = split(h[...])
    refs[-2][...] = hi
    refs[-1][...] = lo


def halves(h, wait_for):
    rows = h.shape[0] // 4 if h.shape[0] % 64 == 0 else h.shape[0]
    spec = pl.BlockSpec((rows, h.shape[1]), lambda i: (i, 0))
    shape = jax.ShapeDtypeStruct(h.shape, jnp.bfloat16)
    return pl.pallas_call(
        halves_kernel,
        grid=(h.shape[0] // rows,),
        in_specs=[spec] + [pl.BlockSpec(memory_space=pl.ANY)] * len(wait_for),
        out_specs=[spec, spec],
        out_shape=[shape, shape],
        compiler_params=params(24),
        cost_estimate=pl.CostEstimate(flops=1, bytes_accessed=1, transcendentals=0),
    )(h, *wait_for)


def scores_kernel(n, m, masks, h_hi, h_lo, *refs):
    queries, grads, out, a = refs[:n], refs[n : 2 * n], refs[2 * n], refs[2 * n + 1]
    half = R // n // 2
    rows = n * n * m
    for s in range(n * n):
        y = grads[s // n][s % n].astype(jnp.float32)
        top = y[half * m :]
        w = root(y[: half * m]) * (1.0 / TOP)
        for r in range(half):
            a[pl.ds(s * m, m), pl.ds(r * LANES, LANES)] = w[r * m : (r + 1) * m] * top
    contract = (((1,), (0,)), ((), ()))
    hi, lo = split(a[...])
    top = lax.dot_general(jnp.concatenate([hi, lo], 0), h_hi[...], contract, preferred_element_type=jnp.float32)
    low = lax.dot_general(hi, h_lo[...], contract, preferred_element_type=jnp.float32)
    hi, lo = split(top[:rows] + top[rows:] + low)
    both = jnp.concatenate([hi, lo], 0)
    d, t = lax.axis_index("dp"), lax.axis_index("tensor")
    for mask, ref in zip(masks, queries):
        to = lax.bitwise_xor(d, mask)
        s = lax.dot_general(both, ref[...], ROWS_CONTRACT, preferred_element_type=jnp.float32)
        s = s[:rows] + s[rows:]
        for p in range(n):
            for b in range(n):
                at = (p * n + b) * m
                back = bitrev(b, n.bit_length() - 1)
                out[back & 1, lax.bitwise_xor(d >> 1, back >> 1), to, lax.bitwise_xor(t, p)] = s[at : at + m]


def scores_of(h_hi, h_lo, queries, grads, n, m):
    masks = sorted(queries)
    blocks = [queries[k] for k in masks]
    width = blocks[0].shape[0]
    return pl.pallas_call(
        functools.partial(scores_kernel, n, m, masks),
        in_specs=[pl.BlockSpec(memory_space=pltpu.VMEM)] * (2 + 2 * n),
        out_specs=pl.BlockSpec(memory_space=pltpu.VMEM),
        out_shape=jax.ShapeDtypeStruct((2, n // 2, n, n, m, width), jnp.float32),
        scratch_shapes=[pltpu.VMEM((n * n * m, R // n // 2 * LANES), jnp.float32)],
        compiler_params=params(40),
    )(h_hi, h_lo, *blocks, *grads)


def local(n, activations, out_grads, proj_in, proj_out, hess_inv, queries):
    bits = n.bit_length() - 1
    examples = activations.shape[0] // SEQ
    m = -(-examples // n)
    def along(v, mask):
        return lax.ppermute(v, "tensor", [(i, i ^ mask) for i in range(n)])

    def flip(v, mask):
        return lax.ppermute(v, "dp", [(i, i ^ mask) for i in range(n)])

    def after(v, first):
        return lax.optimization_barrier((v, first))[0]

    all_q = {0: queries}
    all_q[n // 2] = flip(queries, n // 2)

    far = list(range(n - 1, 1, -1))
    y = project(activations, out_grads, proj_in, proj_out, far, m, 59)
    (near,) = project(activations, after(out_grads, y), proj_in, proj_out, [1], m, 59)
    (own,) = project(activations, after(out_grads, near), proj_in, proj_out, [0], m, 57)
    coded = [along(v, mask) for v, mask in zip(y, far)] + [along(near, 1)]
    grads = grads_of(own * TOP, coded, n, m, bits)
    h_hi, h_lo = halves(hess_inv, [grads, all_q[n // 2]])
    parts = [flip(grads[p], bitrev(p, bits)) for p in range(1, n)]
    first, h_hi, h_lo = lax.optimization_barrier((grads[0], h_hi, h_lo))
    group = jnp.stack([first] + parts)
    groups = [group] + [along(group, s) for s in range(1, n)]
    for b in reversed(range(bits - 1)):
        all_q = dict(zip(all_q, after(tuple(all_q.values()), grads)))
        all_q.update({k | (1 << b): flip(v, 1 << b) for k, v in all_q.items()})

    out = scores_of(h_hi, h_lo, all_q, groups, n, m)
    out = out[0] + flip(out[1], 1)
    same_core = [[(2 * x + core) * n + t for x in range(n // 2) for t in range(n)] for core in range(2)]
    out = out.reshape(n * n // 2, n, m, out.shape[-1])
    out = lax.all_to_all(out, ("dp", "tensor"), 0, 0, tiled=True, axis_index_groups=same_core)
    total = jnp.sum(out, 0)
    width = total.shape[-1]
    total = total.reshape(n * m, width)
    rows, i = [], 0
    while i < examples:
        owner = min(i // m, n - 1)
        begin = min(owner * m, examples - m)
        stop = begin + m
        rows.append(total[owner * m + i - begin : owner * m + stop - begin])
        i = stop
    scale = (1.0 / math.sqrt(SEQ)) * (1.0 / math.sqrt(R * R)) / (TOP * TOP)
    return jnp.concatenate(rows, 0)[:examples] * scale


def solution(mesh):
    n = mesh.shape["tensor"]
    return jax.shard_map(
        functools.partial(local, n),
        mesh=mesh,
        in_specs=(
            P(("groups", "dp"), "tensor"),
            P(("groups", "dp"), "tensor"),
            P(None, "tensor"),
            P(None, "tensor"),
            P("dp", "tensor"),
            P("dp", "tensor"),
        ),
        out_specs=P(("groups", "dp"), "tensor"),
        check_vma=False,
    )
```

```python
import functools
import math

import jax
import jax.numpy as jnp
from jax import lax
from jax.experimental import pallas as pl
from jax.experimental.pallas import tpu as pltpu
from jax.sharding import PartitionSpec as P

R = 64
SEQ = 128
LANES = 128
TOP = 8.0
FLOOR = 0.07
ROWS_CONTRACT = (((1,), (1,)), ((), ()))


def params(mib):
    return pltpu.CompilerParams(vmem_limit_bytes=mib << 20)


def first_example(owner, m, examples):
    return jnp.minimum(owner * m, examples - m)


def bitrev(v, bits):
    out = 0
    for b in range(bits):
        out = out + ((v >> b) & 1) * (1 << (bits - 1 - b))
    return out


def power(x, top):
    w = jnp.abs(x) * (TOP / top) + FLOOR
    s = w * w
    s = s * s
    s = s * s
    s = s * s
    s = s * s
    return jnp.where(x < 0, -s, s)


def root(y):
    s = lax.rsqrt(lax.rsqrt(lax.rsqrt(lax.rsqrt(jnp.abs(y)))))
    w = s * lax.rsqrt(s) - FLOOR
    return jnp.where(y < 0, -w, w)


def column_top(x):
    top = jnp.maximum(jnp.max(jnp.abs(x), axis=0, keepdims=True), 1e-30)
    return top.astype(jnp.bfloat16).astype(jnp.float32)


def encode(x, y_ref):
    rows = x.shape[0]
    top = column_top(x)
    y_ref[pl.ds(0, rows), :] = power(x, top).astype(jnp.bfloat16)
    y_ref[pl.ds(rows, 16), :] = jnp.broadcast_to(top, (16, LANES)).astype(jnp.bfloat16)


def project_kernel(masks, acts, outs, p_in, p_out, *refs):
    y_refs, acc = refs[:-1], refs[-1]
    right = lax.dot_general(acts[...], p_in[...], ROWS_CONTRACT, preferred_element_type=jnp.float32)
    left = lax.dot_general(outs[...], p_out[...], ROWS_CONTRACT, preferred_element_type=jnp.float32)
    acc[...] = jnp.concatenate([left, right], 1)

    def finish(mask, y_ref):
        if mask == 0:
            y_ref[...] = acc[...]
        else:
            encode(acc[...], y_ref)

    for i, (mask, y_ref) in enumerate(zip(masks, y_refs)):
        pl.when(pl.program_id(0) == i)(functools.partial(finish, mask, y_ref))


def project(acts, outs, p_in, p_out, masks, m, mib):
    examples = acts.shape[0] // SEQ
    rows = m * SEQ
    first = masks[0]

    def start(i):
        return first_example(lax.bitwise_xor(lax.axis_index("tensor"), first + i), m, examples) * SEQ

    shapes = [
        jax.ShapeDtypeStruct((rows + 16, LANES), jnp.bfloat16) if k else jax.ShapeDtypeStruct((rows, LANES), jnp.float32)
        for k in masks
    ]
    return pl.pallas_call(
        functools.partial(project_kernel, masks),
        grid=(len(masks),),
        in_specs=[
            pl.BlockSpec((pl.Element(rows), pl.Element(acts.shape[1])), lambda i: (start(i), 0)),
            pl.BlockSpec((pl.Element(rows), pl.Element(outs.shape[1])), lambda i: (start(i), 0)),
            pl.BlockSpec(p_in.shape, lambda i: (0, 0)),
            pl.BlockSpec(p_out.shape, lambda i: (0, 0)),
        ],
        out_specs=[pl.BlockSpec(s.shape, lambda i: (0, 0)) for s in shapes],
        scratch_shapes=[pltpu.VMEM((rows, LANES), jnp.float32)],
        out_shape=shapes,
        compiler_params=params(mib),
        cost_estimate=pl.CostEstimate(flops=1, bytes_accessed=1, transcendentals=0),
    )(acts, outs, p_in, p_out)


def split(v):
    hi = v.astype(jnp.bfloat16)
    return hi, (v - hi.astype(jnp.float32)).astype(jnp.bfloat16)


def grads_kernel(n, m, bits, own, *refs):
    coded, out, z, block = refs[: n - 1], *refs[-3:]
    rows = m * SEQ
    x = own[...]
    for ref in coded:
        y = ref[...].astype(jnp.float32)
        x = x + root(y[:rows]) * y[rows : rows + 1]
    half = R // n // 2
    d = lax.axis_index("dp")
    contract = (((1,), (0,)), ((), ()))
    for e in range(m):
        xe = x[e * SEQ : (e + 1) * SEQ, :]
        hi, lo = split(xe)
        hi_t, lo_t = split(xe.T)
        first = lax.dot_general(jnp.concatenate([hi_t, lo_t], 0), hi, contract, preferred_element_type=jnp.float32)
        last = lax.dot_general(hi_t, lo, contract, preferred_element_type=jnp.float32)
        z[e] = first[:LANES] + first[LANES:] + last
    for j in range(n):
        for e in range(m):
            even = z[e, pl.ds(2 * half * j, half, stride=2), :]
            odd = z[e, pl.ds(2 * half * j + 1, half, stride=2), :]
            g = jnp.concatenate([even[:, R:], odd[:, R:]], 1)
            top = column_top(g)
            block[pl.ds(e, half, stride=m), :] = power(g, top)
            block[pl.ds(half * m + e, 1), :] = top
        out[bitrev(lax.bitwise_xor(d, j), bits)] = block[...].astype(jnp.bfloat16)


def grads_of(own, coded, n, m, bits):
    rows = (R // n // 2 + 1) * m
    return pl.pallas_call(
        functools.partial(grads_kernel, n, m, bits),
        in_specs=[pl.BlockSpec(memory_space=pltpu.VMEM)] * n,
        out_specs=pl.BlockSpec(memory_space=pltpu.VMEM),
        out_shape=jax.ShapeDtypeStruct((n, rows, LANES), jnp.bfloat16),
        scratch_shapes=[pltpu.VMEM((m, SEQ, LANES), jnp.float32), pltpu.VMEM((rows, LANES), jnp.float32)],
        compiler_params=params(24),
        cost_estimate=pl.CostEstimate(flops=1, bytes_accessed=1, transcendentals=0),
    )(own, *coded)


def halves_kernel(h, *refs):
    hi, lo = split(h[...])
    refs[-2][...] = hi
    refs[-1][...] = lo


def halves(h, wait_for):
    rows = h.shape[0] // 4 if h.shape[0] % 64 == 0 else h.shape[0]
    spec = pl.BlockSpec((rows, h.shape[1]), lambda i: (i, 0))
    shape = jax.ShapeDtypeStruct(h.shape, jnp.bfloat16)
    return pl.pallas_call(
        halves_kernel,
        grid=(h.shape[0] // rows,),
        in_specs=[spec] + [pl.BlockSpec(memory_space=pl.ANY)] * len(wait_for),
        out_specs=[spec, spec],
        out_shape=[shape, shape],
        compiler_params=params(24),
        cost_estimate=pl.CostEstimate(flops=1, bytes_accessed=1, transcendentals=0),
    )(h, *wait_for)


def scores_kernel(n, m, masks, h_hi, h_lo, *refs):
    queries, grads, out, a = refs[:n], refs[n : 2 * n], refs[2 * n], refs[2 * n + 1]
    half = R // n // 2
    rows = n * n * m
    for s in range(n * n):
        y = grads[s // n][s % n].astype(jnp.float32)
        top = y[half * m :]
        w = root(y[: half * m]) * (1.0 / TOP)
        for r in range(half):
            a[pl.ds(s * m, m), pl.ds(r * LANES, LANES)] = w[r * m : (r + 1) * m] * top
    contract = (((1,), (0,)), ((), ()))
    hi, lo = split(a[...])
    top = lax.dot_general(jnp.concatenate([hi, lo], 0), h_hi[...], contract, preferred_element_type=jnp.float32)
    low = lax.dot_general(hi, h_lo[...], contract, preferred_element_type=jnp.float32)
    hi, lo = split(top[:rows] + top[rows:] + low)
    both = jnp.concatenate([hi, lo], 0)
    d, t = lax.axis_index("dp"), lax.axis_index("tensor")
    for mask, ref in zip(masks, queries):
        to = lax.bitwise_xor(d, mask)
        s = lax.dot_general(both, ref[...], ROWS_CONTRACT, preferred_element_type=jnp.float32)
        s = s[:rows] + s[rows:]
        for p in range(n):
            for b in range(n):
                at = (p * n + b) * m
                back = bitrev(b, n.bit_length() - 1)
                out[back & 1, lax.bitwise_xor(d >> 1, back >> 1), to, lax.bitwise_xor(t, p)] = s[at : at + m]


def scores_of(h_hi, h_lo, queries, grads, n, m):
    masks = sorted(queries)
    blocks = [queries[k] for k in masks]
    width = blocks[0].shape[0]
    return pl.pallas_call(
        functools.partial(scores_kernel, n, m, masks),
        in_specs=[pl.BlockSpec(memory_space=pltpu.VMEM)] * (2 + 2 * n),
        out_specs=pl.BlockSpec(memory_space=pltpu.VMEM),
        out_shape=jax.ShapeDtypeStruct((2, n // 2, n, n, m, width), jnp.float32),
        scratch_shapes=[pltpu.VMEM((n * n * m, R // n // 2 * LANES), jnp.float32)],
        compiler_params=params(40),
    )(h_hi, h_lo, *blocks, *grads)


def each(count, body):
    if count <= 8:
        for i in range(count):
            body(i)
    else:
        lax.fori_loop(0, count, lambda i, c: (body(i), c)[1], 0)


def pack_kernel(n, m, examples, ours, theirs, out):
    def one(i):
        x, t = i // n, i % n
        rows, done = [], 0
        while done < examples:
            owner = min(done // m, n - 1)
            begin = min(owner * m, examples - m)
            both = ours[0, x, t, owner] + theirs[x, t, owner]
            rows.append(both[done - begin :])
            done = begin + m
        both = jnp.concatenate(rows, 0)
        top = column_top(both)
        out[i] = jnp.concatenate([power(both, top), top], 0).astype(jnp.bfloat16)

    each(n * n // 2, one)


def pack(ours, theirs, n, m, examples):
    width = ours.shape[-1]
    return pl.pallas_call(
        functools.partial(pack_kernel, n, m, examples),
        in_specs=[pl.BlockSpec(memory_space=pltpu.VMEM)] * 2,
        out_specs=pl.BlockSpec(memory_space=pltpu.VMEM),
        out_shape=jax.ShapeDtypeStruct((n * n // 2, examples + 1, width), jnp.bfloat16),
        compiler_params=params(40),
    )(ours, theirs)


def unpack_kernel(examples, scale, y_ref, out):
    def term(i):
        y = y_ref[i].astype(jnp.float32)
        return root(y[:examples]) * y[examples:]

    count = y_ref.shape[0]
    if count <= 8:
        total = sum(term(i) for i in range(count))
    else:
        total = lax.fori_loop(1, count, lambda i, c: c + term(i), term(0))
    out[...] = total * scale


def unpack(y, scale):
    examples = y.shape[1] - 1
    return pl.pallas_call(
        functools.partial(unpack_kernel, examples, scale),
        in_specs=[pl.BlockSpec(memory_space=pltpu.VMEM)],
        out_specs=pl.BlockSpec(memory_space=pltpu.VMEM),
        out_shape=jax.ShapeDtypeStruct((examples, y.shape[2]), jnp.float32),
        compiler_params=params(24),
    )(y)


def local(n, activations, out_grads, proj_in, proj_out, hess_inv, queries):
    bits = n.bit_length() - 1
    examples = activations.shape[0] // SEQ
    m = -(-examples // n)
    def along(v, mask):
        return lax.ppermute(v, "tensor", [(i, i ^ mask) for i in range(n)])

    def flip(v, mask):
        return lax.ppermute(v, "dp", [(i, i ^ mask) for i in range(n)])

    def after(v, first):
        return lax.optimization_barrier((v, first))[0]

    all_q = {0: queries}
    all_q[n // 2] = flip(queries, n // 2)

    far = list(range(2, n))
    y = project(activations, out_grads, proj_in, proj_out, far, m, 59)
    (near,) = project(activations, after(out_grads, y), proj_in, proj_out, [1], m, 59)
    (own,) = project(activations, after(out_grads, near), proj_in, proj_out, [0], m, 57)
    coded = [along(v, mask) for v, mask in zip(y, far)] + [along(near, 1)]
    grads = grads_of(own * TOP, coded, n, m, bits)
    h_hi, h_lo = halves(hess_inv, [grads, all_q[n // 2]])
    parts = [flip(grads[p], bitrev(p, bits)) for p in range(1, n)]
    first, h_hi, h_lo = lax.optimization_barrier((grads[0], h_hi, h_lo))
    group = jnp.stack([first] + parts)
    groups = [group] + [along(group, s) for s in range(1, n)]
    for b in reversed(range(bits - 1)):
        all_q = dict(zip(all_q, after(tuple(all_q.values()), grads)))
        all_q.update({k | (1 << b): flip(v, 1 << b) for k, v in all_q.items()})

    out = scores_of(h_hi, h_lo, all_q, groups, n, m)
    out = pack(out, flip(out[1], 1), n, m, examples)
    same_core = [[(2 * x + core) * n + t for x in range(n // 2) for t in range(n)] for core in range(2)]
    out = lax.all_to_all(out, ("dp", "tensor"), 0, 0, tiled=True, axis_index_groups=same_core)
    return unpack(out, (1.0 / math.sqrt(SEQ)) * (1.0 / math.sqrt(R * R)) / (TOP * TOP) / TOP)


def solution(mesh):
    n = mesh.shape["tensor"]
    return jax.shard_map(
        functools.partial(local, n),
        mesh=mesh,
        in_specs=(
            P(("groups", "dp"), "tensor"),
            P(("groups", "dp"), "tensor"),
            P(None, "tensor"),
            P(None, "tensor"),
            P("dp", "tensor"),
            P("dp", "tensor"),
        ),
        out_specs=P(("groups", "dp"), "tensor"),
        check_vma=False,
    )
```

```python
import functools
import math

import jax
import jax.numpy as jnp
from jax import lax
from jax.experimental import pallas as pl
from jax.experimental.pallas import tpu as pltpu
from jax.sharding import PartitionSpec as P

R = 64
SEQ = 128
LANES = 128
TOP = 8.0
FLOOR = 0.07
ROWS_CONTRACT = (((1,), (1,)), ((), ()))


def params(mib):
    return pltpu.CompilerParams(vmem_limit_bytes=mib << 20)


def first_example(owner, m, examples):
    return jnp.minimum(owner * m, examples - m)


def bitrev(v, bits):
    out = 0
    for b in range(bits):
        out = out + ((v >> b) & 1) * (1 << (bits - 1 - b))
    return out


def power(x, top):
    w = jnp.abs(x) * (TOP / top) + FLOOR
    s = w * w
    s = s * s
    s = s * s
    s = s * s
    s = s * s
    return jnp.where(x < 0, -s, s)


def root(y):
    s = lax.rsqrt(lax.rsqrt(lax.rsqrt(lax.rsqrt(jnp.abs(y)))))
    w = s * lax.rsqrt(s) - FLOOR
    return jnp.where(y < 0, -w, w)


def column_top(x):
    top = jnp.maximum(jnp.max(jnp.abs(x), axis=0, keepdims=True), 1e-30)
    return top.astype(jnp.bfloat16).astype(jnp.float32)


def encode(x, y_ref):
    rows = x.shape[0]
    top = column_top(x)
    y_ref[pl.ds(0, rows), :] = power(x, top).astype(jnp.bfloat16)
    y_ref[pl.ds(rows, 16), :] = jnp.broadcast_to(top, (16, LANES)).astype(jnp.bfloat16)


def project_kernel(masks, acts, outs, p_in, p_out, *refs):
    y_refs, acc = refs[:-1], refs[-1]
    right = lax.dot_general(acts[...], p_in[...], ROWS_CONTRACT, preferred_element_type=jnp.float32)
    left = lax.dot_general(outs[...], p_out[...], ROWS_CONTRACT, preferred_element_type=jnp.float32)
    acc[...] = jnp.concatenate([left, right], 1)

    def finish(mask, y_ref):
        if mask == 0:
            y_ref[...] = acc[...]
        else:
            encode(acc[...], y_ref)

    for i, (mask, y_ref) in enumerate(zip(masks, y_refs)):
        pl.when(pl.program_id(0) == i)(functools.partial(finish, mask, y_ref))


def project(acts, outs, p_in, p_out, masks, m, mib):
    examples = acts.shape[0] // SEQ
    rows = m * SEQ
    first = masks[0]

    def start(i):
        return first_example(lax.bitwise_xor(lax.axis_index("tensor"), first + i), m, examples) * SEQ

    shapes = [
        jax.ShapeDtypeStruct((rows + 16, LANES), jnp.bfloat16) if k else jax.ShapeDtypeStruct((rows, LANES), jnp.float32)
        for k in masks
    ]
    return pl.pallas_call(
        functools.partial(project_kernel, masks),
        grid=(len(masks),),
        in_specs=[
            pl.BlockSpec((pl.Element(rows), pl.Element(acts.shape[1])), lambda i: (start(i), 0)),
            pl.BlockSpec((pl.Element(rows), pl.Element(outs.shape[1])), lambda i: (start(i), 0)),
            pl.BlockSpec(p_in.shape, lambda i: (0, 0)),
            pl.BlockSpec(p_out.shape, lambda i: (0, 0)),
        ],
        out_specs=[pl.BlockSpec(s.shape, lambda i: (0, 0)) for s in shapes],
        scratch_shapes=[pltpu.VMEM((rows, LANES), jnp.float32)],
        out_shape=shapes,
        compiler_params=params(mib),
        cost_estimate=pl.CostEstimate(flops=1, bytes_accessed=1, transcendentals=0),
    )(acts, outs, p_in, p_out)


def split(v):
    hi = v.astype(jnp.bfloat16)
    return hi, (v - hi.astype(jnp.float32)).astype(jnp.bfloat16)


def grads_kernel(n, m, own, *refs):
    coded, out, z, block = refs[: n - 1], *refs[-3:]
    rows = m * SEQ
    x = own[...]
    for ref in coded:
        y = ref[...].astype(jnp.float32)
        x = x + root(y[:rows]) * y[rows : rows + 1]
    half = R // n // 2
    contract = (((1,), (0,)), ((), ()))
    for e in range(m):
        xe = x[e * SEQ : (e + 1) * SEQ, :]
        hi, lo = split(xe)
        hi_t, lo_t = split(xe.T)
        first = lax.dot_general(jnp.concatenate([hi_t, lo_t], 0), hi, contract, preferred_element_type=jnp.float32)
        last = lax.dot_general(hi_t, lo, contract, preferred_element_type=jnp.float32)
        z[e] = first[:LANES] + first[LANES:] + last
    for j in range(n):
        for e in range(m):
            even = z[e, pl.ds(2 * half * j, half, stride=2), :]
            odd = z[e, pl.ds(2 * half * j + 1, half, stride=2), :]
            g = jnp.concatenate([even[:, R:], odd[:, R:]], 1)
            top = column_top(g)
            block[pl.ds(e, half, stride=m), :] = power(g, top)
            block[pl.ds(half * m + e, 1), :] = top
        y = block[...].astype(jnp.bfloat16)
        for t in range(n):
            out[j * n + t] = y


def grads_of(own, coded, wait_for, n, m):
    rows = (R // n // 2 + 1) * m
    return pl.pallas_call(
        functools.partial(grads_kernel, n, m),
        in_specs=[pl.BlockSpec(memory_space=pltpu.VMEM)] * n + [pl.BlockSpec(memory_space=pl.ANY)] * len(wait_for),
        out_specs=pl.BlockSpec(memory_space=pltpu.VMEM),
        out_shape=jax.ShapeDtypeStruct((n * n, rows, LANES), jnp.bfloat16),
        scratch_shapes=[pltpu.VMEM((m, SEQ, LANES), jnp.float32), pltpu.VMEM((rows, LANES), jnp.float32)],
        compiler_params=params(24),
        cost_estimate=pl.CostEstimate(flops=1, bytes_accessed=1, transcendentals=0),
    )(own, *coded, *wait_for)


def halves_kernel(h, *refs):
    hi, lo = split(h[...])
    refs[-2][...] = hi
    refs[-1][...] = lo


def halves(h, wait_for):
    rows = h.shape[0] // 4 if h.shape[0] % 64 == 0 else h.shape[0]
    spec = pl.BlockSpec((rows, h.shape[1]), lambda i: (i, 0))
    shape = jax.ShapeDtypeStruct(h.shape, jnp.bfloat16)
    return pl.pallas_call(
        halves_kernel,
        grid=(h.shape[0] // rows,),
        in_specs=[spec] + [pl.BlockSpec(memory_space=pl.ANY)] * len(wait_for),
        out_specs=[spec, spec],
        out_shape=[shape, shape],
        compiler_params=params(24),
        cost_estimate=pl.CostEstimate(flops=1, bytes_accessed=1, transcendentals=0),
    )(h, *wait_for)


def scores_kernel(n, m, masks, h_hi, h_lo, *refs):
    grads, queries, out, a = refs[0], refs[1 : n + 1], refs[n + 1], refs[n + 2]
    half = R // n // 2
    rows = n * n * m
    for s in range(n * n):
        y = grads[s].astype(jnp.float32)
        top = y[half * m :]
        w = root(y[: half * m]) * (1.0 / TOP)
        for r in range(half):
            a[pl.ds(s * m, m), pl.ds(r * LANES, LANES)] = w[r * m : (r + 1) * m] * top
    contract = (((1,), (0,)), ((), ()))
    hi, lo = split(a[...])
    top = lax.dot_general(jnp.concatenate([hi, lo], 0), h_hi[...], contract, preferred_element_type=jnp.float32)
    low = lax.dot_general(hi, h_lo[...], contract, preferred_element_type=jnp.float32)
    hi, lo = split(top[:rows] + top[rows:] + low)
    both = jnp.concatenate([hi, lo], 0)
    d = lax.axis_index("dp")
    for mask, ref in zip(masks, queries):
        to = lax.bitwise_xor(d, mask)
        s = lax.dot_general(both, ref[...], ROWS_CONTRACT, preferred_element_type=jnp.float32)
        s = s[:rows] + s[rows:]
        for p in range(n):
            for b in range(n):
                at = (p * n + b) * m
                out[lax.bitwise_xor(d, p) & 1, p >> 1, to, b] = s[at : at + m]


def scores_of(h_hi, h_lo, queries, grads, n, m):
    masks = sorted(queries)
    blocks = [queries[k] for k in masks]
    width = blocks[0].shape[0]
    return pl.pallas_call(
        functools.partial(scores_kernel, n, m, masks),
        in_specs=[pl.BlockSpec(memory_space=pltpu.VMEM)] * (3 + n),
        out_specs=pl.BlockSpec(memory_space=pltpu.VMEM),
        out_shape=jax.ShapeDtypeStruct((2, n // 2, n, n, m, width), jnp.float32),
        scratch_shapes=[pltpu.VMEM((n * n * m, R // n // 2 * LANES), jnp.float32)],
        compiler_params=params(40),
    )(h_hi, h_lo, grads, *blocks)


def each(count, body):
    if count <= 8:
        for i in range(count):
            body(i)
    else:
        lax.fori_loop(0, count, lambda i, c: (body(i), c)[1], 0)


def pack_kernel(n, m, examples, ours, theirs, out):
    def one(i):
        x, t = i // n, i % n
        rows, done = [], 0
        while done < examples:
            owner = min(done // m, n - 1)
            begin = min(owner * m, examples - m)
            both = ours[0, x, t, owner] + theirs[x, t, owner]
            rows.append(both[done - begin :])
            done = begin + m
        both = jnp.concatenate(rows, 0)
        top = column_top(both)
        out[i] = jnp.concatenate([power(both, top), top], 0).astype(jnp.bfloat16)

    each(n * n // 2, one)


def pack(ours, theirs, n, m, examples):
    width = ours.shape[-1]
    return pl.pallas_call(
        functools.partial(pack_kernel, n, m, examples),
        in_specs=[pl.BlockSpec(memory_space=pltpu.VMEM)] * 2,
        out_specs=pl.BlockSpec(memory_space=pltpu.VMEM),
        out_shape=jax.ShapeDtypeStruct((n * n // 2, examples + 1, width), jnp.bfloat16),
        compiler_params=params(40),
    )(ours, theirs)


def unpack_kernel(examples, scale, y_ref, out):
    def term(i):
        y = y_ref[i].astype(jnp.float32)
        return root(y[:examples]) * y[examples:]

    count = y_ref.shape[0]
    if count <= 8:
        total = sum(term(i) for i in range(count))
    else:
        total = lax.fori_loop(1, count, lambda i, c: c + term(i), term(0))
    out[...] = total * scale


def unpack(y, scale):
    examples = y.shape[1] - 1
    return pl.pallas_call(
        functools.partial(unpack_kernel, examples, scale),
        in_specs=[pl.BlockSpec(memory_space=pltpu.VMEM)],
        out_specs=pl.BlockSpec(memory_space=pltpu.VMEM),
        out_shape=jax.ShapeDtypeStruct((examples, y.shape[2]), jnp.float32),
        compiler_params=params(24),
    )(y)


def local(n, activations, out_grads, proj_in, proj_out, hess_inv, queries):
    bits = n.bit_length() - 1
    examples = activations.shape[0] // SEQ
    m = -(-examples // n)
    def along(v, mask):
        return lax.ppermute(v, "tensor", [(i, i ^ mask) for i in range(n)])

    def flip(v, mask):
        return lax.ppermute(v, "dp", [(i, i ^ mask) for i in range(n)])

    def after(v, first):
        return lax.optimization_barrier((v, first))[0]

    all_q = {0: queries}
    all_q[n // 2] = flip(queries, n // 2)

    far = list(range(2, n))
    y = project(activations, out_grads, proj_in, proj_out, far, m, 59)
    (near,) = project(activations, after(out_grads, y), proj_in, proj_out, [1], m, 59)
    (own,) = project(activations, after(out_grads, near), proj_in, proj_out, [0], m, 57)
    coded = [along(v, mask) for v, mask in zip(y, far)] + [along(near, 1)]
    h_hi, h_lo = halves(hess_inv, [own])
    grads = grads_of(own * TOP, coded, [h_hi, all_q[n // 2]], n, m)
    for b in reversed(range(bits - 1)):
        all_q = dict(zip(all_q, after(tuple(all_q.values()), grads)))
        all_q.update({k | (1 << b): flip(v, 1 << b) for k, v in all_q.items()})

    grads_all = lax.all_to_all(grads, ("dp", "tensor"), 0, 0, tiled=True)
    out = scores_of(h_hi, h_lo, all_q, grads_all, n, m)
    out = pack(out, flip(out[1], 1), n, m, examples)
    same_core = [[(2 * x + core) * n + t for x in range(n // 2) for t in range(n)] for core in range(2)]
    out = lax.all_to_all(out, ("dp", "tensor"), 0, 0, tiled=True, axis_index_groups=same_core)
    return unpack(out, (1.0 / math.sqrt(SEQ)) * (1.0 / math.sqrt(R * R)) / (TOP * TOP) / TOP)


def solution(mesh):
    n = mesh.shape["tensor"]
    return jax.shard_map(
        functools.partial(local, n),
        mesh=mesh,
        in_specs=(
            P(("groups", "dp"), "tensor"),
            P(("groups", "dp"), "tensor"),
            P(None, "tensor"),
            P(None, "tensor"),
            P("dp", "tensor"),
            P("dp", "tensor"),
        ),
        out_specs=P(("groups", "dp"), "tensor"),
        check_vma=False,
    )
```

```python
import functools
import math

import jax
import jax.numpy as jnp
from jax import lax
from jax.experimental import pallas as pl
from jax.experimental.pallas import tpu as pltpu
from jax.sharding import PartitionSpec as P

R = 64
SEQ = 128
LANES = 128
TOP = 8.0
FLOOR = 0.07
ROWS_CONTRACT = (((1,), (1,)), ((), ()))


def params(mib):
    return pltpu.CompilerParams(vmem_limit_bytes=mib << 20)


def first_example(owner, m, examples):
    return jnp.minimum(owner * m, examples - m)


def bitrev(v, bits):
    out = 0
    for b in range(bits):
        out = out + ((v >> b) & 1) * (1 << (bits - 1 - b))
    return out


def power(x, top):
    w = jnp.abs(x) * (TOP / top) + FLOOR
    s = w * w
    s = s * s
    s = s * s
    s = s * s
    s = s * s
    return jnp.where(x < 0, -s, s)


def root(y):
    s = lax.rsqrt(lax.rsqrt(lax.rsqrt(lax.rsqrt(jnp.abs(y)))))
    w = s * lax.rsqrt(s) - FLOOR
    return jnp.where(y < 0, -w, w)


def column_top(x):
    top = jnp.maximum(jnp.max(jnp.abs(x), axis=0, keepdims=True), 1e-30)
    return top.astype(jnp.bfloat16).astype(jnp.float32)


def encode(x, y_ref):
    rows = x.shape[0]
    top = column_top(x)
    y_ref[pl.ds(0, rows), :] = power(x, top).astype(jnp.bfloat16)
    y_ref[pl.ds(rows, 16), :] = jnp.broadcast_to(top, (16, LANES)).astype(jnp.bfloat16)


def project_kernel(masks, acts, outs, p_in, p_out, *refs):
    y_refs, acc = refs[:-1], refs[-1]
    right = lax.dot_general(acts[...], p_in[...], ROWS_CONTRACT, preferred_element_type=jnp.float32)
    left = lax.dot_general(outs[...], p_out[...], ROWS_CONTRACT, preferred_element_type=jnp.float32)
    acc[...] = jnp.concatenate([left, right], 1)

    def finish(mask, y_ref):
        if mask == 0:
            y_ref[...] = acc[...]
        else:
            encode(acc[...], y_ref)

    for i, (mask, y_ref) in enumerate(zip(masks, y_refs)):
        pl.when(pl.program_id(0) == i)(functools.partial(finish, mask, y_ref))


def project(acts, outs, p_in, p_out, masks, m, mib):
    examples = acts.shape[0] // SEQ
    rows = m * SEQ
    first = masks[0]

    def start(i):
        return first_example(lax.bitwise_xor(lax.axis_index("tensor"), first + i), m, examples) * SEQ

    shapes = [
        jax.ShapeDtypeStruct((rows + 16, LANES), jnp.bfloat16) if k else jax.ShapeDtypeStruct((rows, LANES), jnp.float32)
        for k in masks
    ]
    return pl.pallas_call(
        functools.partial(project_kernel, masks),
        grid=(len(masks),),
        in_specs=[
            pl.BlockSpec((pl.Element(rows), pl.Element(acts.shape[1])), lambda i: (start(i), 0)),
            pl.BlockSpec((pl.Element(rows), pl.Element(outs.shape[1])), lambda i: (start(i), 0)),
            pl.BlockSpec(p_in.shape, lambda i: (0, 0)),
            pl.BlockSpec(p_out.shape, lambda i: (0, 0)),
        ],
        out_specs=[pl.BlockSpec(s.shape, lambda i: (0, 0)) for s in shapes],
        scratch_shapes=[pltpu.VMEM((rows, LANES), jnp.float32)],
        out_shape=shapes,
        compiler_params=params(mib),
        cost_estimate=pl.CostEstimate(flops=1, bytes_accessed=1, transcendentals=0),
    )(acts, outs, p_in, p_out)


def split(v):
    hi = v.astype(jnp.bfloat16)
    return hi, (v - hi.astype(jnp.float32)).astype(jnp.bfloat16)


def grads_kernel(n, m, own, *refs):
    coded, out, z, block = refs[: n - 1], *refs[-3:]
    rows = m * SEQ
    x = own[...]
    for ref in coded:
        y = ref[...].astype(jnp.float32)
        x = x + root(y[:rows]) * y[rows : rows + 1]
    half = R // n // 2
    contract = (((1,), (0,)), ((), ()))
    for e in range(m):
        xe = x[e * SEQ : (e + 1) * SEQ, :]
        hi, lo = split(xe)
        hi_t, lo_t = split(xe.T)
        first = lax.dot_general(jnp.concatenate([hi_t, lo_t], 0), hi, contract, preferred_element_type=jnp.float32)
        last = lax.dot_general(hi_t, lo, contract, preferred_element_type=jnp.float32)
        z[e] = first[:LANES] + first[LANES:] + last
    for j in range(n):
        for e in range(m):
            even = z[e, pl.ds(2 * half * j, half, stride=2), :]
            odd = z[e, pl.ds(2 * half * j + 1, half, stride=2), :]
            g = jnp.concatenate([even[:, R:], odd[:, R:]], 1)
            top = column_top(g)
            block[pl.ds(e, half, stride=m), :] = power(g, top)
            block[pl.ds(half * m + e, 1), :] = top
        y = block[...].astype(jnp.bfloat16)
        for t in range(n):
            out[j * n + t] = y


def grads_of(own, coded, wait_for, n, m):
    rows = (R // n // 2 + 1) * m
    return pl.pallas_call(
        functools.partial(grads_kernel, n, m),
        in_specs=[pl.BlockSpec(memory_space=pltpu.VMEM)] * n + [pl.BlockSpec(memory_space=pl.ANY)] * len(wait_for),
        out_specs=pl.BlockSpec(memory_space=pltpu.VMEM),
        out_shape=jax.ShapeDtypeStruct((n * n, rows, LANES), jnp.bfloat16),
        scratch_shapes=[pltpu.VMEM((m, SEQ, LANES), jnp.float32), pltpu.VMEM((rows, LANES), jnp.float32)],
        compiler_params=params(24),
        cost_estimate=pl.CostEstimate(flops=1, bytes_accessed=1, transcendentals=0),
    )(own, *coded, *wait_for)


def halves_kernel(h, *refs):
    hi, lo = split(h[...])
    refs[-2][...] = hi
    refs[-1][...] = lo


def halves(h, wait_for):
    rows = h.shape[0] // 4 if h.shape[0] % 64 == 0 else h.shape[0]
    spec = pl.BlockSpec((rows, h.shape[1]), lambda i: (i, 0))
    shape = jax.ShapeDtypeStruct(h.shape, jnp.bfloat16)
    return pl.pallas_call(
        halves_kernel,
        grid=(h.shape[0] // rows,),
        in_specs=[spec] + [pl.BlockSpec(memory_space=pl.ANY)] * len(wait_for),
        out_specs=[spec, spec],
        out_shape=[shape, shape],
        compiler_params=params(24),
        cost_estimate=pl.CostEstimate(flops=1, bytes_accessed=1, transcendentals=0),
    )(h, *wait_for)


def scores_kernel(n, m, examples, masks, h_hi, h_lo, *refs):
    grads, queries, out, a = refs[0], refs[1 : n + 1], refs[n + 1], refs[n + 2]
    half = R // n // 2
    rows = n * n * m
    for s in range(n * n):
        y = grads[s].astype(jnp.float32)
        top = y[half * m :]
        w = root(y[: half * m]) * (1.0 / TOP)
        for r in range(half):
            a[pl.ds(s * m, m), pl.ds(r * LANES, LANES)] = w[r * m : (r + 1) * m] * top
    contract = (((1,), (0,)), ((), ()))
    hi, lo = split(a[...])
    top = lax.dot_general(jnp.concatenate([hi, lo], 0), h_hi[...], contract, preferred_element_type=jnp.float32)
    low = lax.dot_general(hi, h_lo[...], contract, preferred_element_type=jnp.float32)
    hi, lo = split(top[:rows] + top[rows:] + low)
    both = jnp.concatenate([hi, lo], 0)
    d = lax.axis_index("dp")
    for mask, ref in zip(masks, queries):
        to = lax.bitwise_xor(d, mask)
        s = lax.dot_general(both, ref[...], ROWS_CONTRACT, preferred_element_type=jnp.float32)
        s = s[:rows] + s[rows:]
        for p in range(n):
            kept, done = [], 0
            while done < examples:
                owner = min(done // m, n - 1)
                begin = min(owner * m, examples - m)
                at = (p * n + owner) * m
                kept.append(s[at + done - begin : at + m])
                done = begin + m
            part = jnp.concatenate(kept, 0)
            top = column_top(part)
            out[p * n + to] = jnp.concatenate([power(part, top), top], 0).astype(jnp.bfloat16)


def scores_of(h_hi, h_lo, queries, grads, n, m, examples):
    masks = sorted(queries)
    blocks = [queries[k] for k in masks]
    width = blocks[0].shape[0]
    return pl.pallas_call(
        functools.partial(scores_kernel, n, m, examples, masks),
        in_specs=[pl.BlockSpec(memory_space=pltpu.VMEM)] * (3 + n),
        out_specs=pl.BlockSpec(memory_space=pltpu.VMEM),
        out_shape=jax.ShapeDtypeStruct((n * n, examples + 1, width), jnp.bfloat16),
        scratch_shapes=[pltpu.VMEM((n * n * m, R // n // 2 * LANES), jnp.float32)],
        compiler_params=params(40),
    )(h_hi, h_lo, grads, *blocks)


def unpack_kernel(examples, scale, y_ref, out):
    def term(i):
        y = y_ref[i].astype(jnp.float32)
        return root(y[:examples]) * y[examples:]

    count = y_ref.shape[0]
    if count <= 16:
        total = sum(term(i) for i in range(count))
    else:
        total = lax.fori_loop(1, count, lambda i, c: c + term(i), term(0))
    out[...] = total * scale


def unpack(y, scale):
    examples = y.shape[1] - 1
    return pl.pallas_call(
        functools.partial(unpack_kernel, examples, scale),
        in_specs=[pl.BlockSpec(memory_space=pltpu.VMEM)],
        out_specs=pl.BlockSpec(memory_space=pltpu.VMEM),
        out_shape=jax.ShapeDtypeStruct((examples, y.shape[2]), jnp.float32),
        compiler_params=params(24),
    )(y)


def local(n, activations, out_grads, proj_in, proj_out, hess_inv, queries):
    bits = n.bit_length() - 1
    examples = activations.shape[0] // SEQ
    m = -(-examples // n)
    def along(v, mask):
        return lax.ppermute(v, "tensor", [(i, i ^ mask) for i in range(n)])

    def flip(v, mask):
        return lax.ppermute(v, "dp", [(i, i ^ mask) for i in range(n)])

    def after(v, first):
        return lax.optimization_barrier((v, first))[0]

    all_q = {0: queries}
    all_q[n // 2] = flip(queries, n // 2)

    far = list(range(2, n))
    y = project(activations, out_grads, proj_in, proj_out, far, m, 59)
    (near,) = project(activations, after(out_grads, y), proj_in, proj_out, [1], m, 59)
    (own,) = project(activations, after(out_grads, near), proj_in, proj_out, [0], m, 57)
    coded = [along(v, mask) for v, mask in zip(y, far)] + [along(near, 1)]
    h_hi, h_lo = halves(hess_inv, [own])
    grads = grads_of(own * TOP, coded, [h_hi, all_q[n // 2]], n, m)
    for b in reversed(range(bits - 1)):
        all_q = dict(zip(all_q, after(tuple(all_q.values()), grads)))
        all_q.update({k | (1 << b): flip(v, 1 << b) for k, v in all_q.items()})

    grads_all = lax.all_to_all(grads, ("dp", "tensor"), 0, 0, tiled=True)
    out = scores_of(h_hi, h_lo, all_q, grads_all, n, m, examples)
    out = lax.all_to_all(out, ("dp", "tensor"), 0, 0, tiled=True)
    return unpack(out, (1.0 / math.sqrt(SEQ)) * (1.0 / math.sqrt(R * R)) / (TOP * TOP) / TOP)


def solution(mesh):
    n = mesh.shape["tensor"]
    return jax.shard_map(
        functools.partial(local, n),
        mesh=mesh,
        in_specs=(
            P(("groups", "dp"), "tensor"),
            P(("groups", "dp"), "tensor"),
            P(None, "tensor"),
            P(None, "tensor"),
            P("dp", "tensor"),
            P("dp", "tensor"),
        ),
        out_specs=P(("groups", "dp"), "tensor"),
        check_vma=False,
    )
```

```python
import functools
import math

import jax
import jax.numpy as jnp
from jax import lax
from jax.experimental import pallas as pl
from jax.experimental.pallas import tpu as pltpu
from jax.sharding import PartitionSpec as P

R = 64
SEQ = 128
LANES = 128
TOP = 8.0
FLOOR = 0.07
ROWS_CONTRACT = (((1,), (1,)), ((), ()))


def params(mib):
    return pltpu.CompilerParams(vmem_limit_bytes=mib << 20)


def first_example(owner, m, examples):
    return jnp.minimum(owner * m, examples - m)


def bitrev(v, bits):
    out = 0
    for b in range(bits):
        out = out + ((v >> b) & 1) * (1 << (bits - 1 - b))
    return out


def power(x, top):
    w = jnp.abs(x) * (TOP / top) + FLOOR
    s = w * w
    s = s * s
    s = s * s
    s = s * s
    s = s * s
    return jnp.where(x < 0, -s, s)


def root(y):
    s = lax.rsqrt(lax.rsqrt(lax.rsqrt(lax.rsqrt(jnp.abs(y)))))
    w = s * lax.rsqrt(s) - FLOOR
    return jnp.where(y < 0, -w, w)


def column_top(x):
    top = jnp.maximum(jnp.max(jnp.abs(x), axis=0, keepdims=True), 1e-30)
    return top.astype(jnp.bfloat16).astype(jnp.float32)


def encode(x, y_ref):
    rows = x.shape[0]
    top = column_top(x)
    y_ref[pl.ds(0, rows), :] = power(x, top).astype(jnp.bfloat16)
    y_ref[pl.ds(rows, 16), :] = jnp.broadcast_to(top, (16, LANES)).astype(jnp.bfloat16)


def project_kernel(masks, acts, outs, p_in, p_out, *refs):
    y_refs, acc = refs[:-1], refs[-1]
    right = lax.dot_general(acts[...], p_in[...], ROWS_CONTRACT, preferred_element_type=jnp.float32)
    left = lax.dot_general(outs[...], p_out[...], ROWS_CONTRACT, preferred_element_type=jnp.float32)
    acc[...] = jnp.concatenate([left, right], 1)

    def finish(mask, y_ref):
        if mask == 0:
            y_ref[...] = acc[...]
        else:
            encode(acc[...], y_ref)

    for i, (mask, y_ref) in enumerate(zip(masks, y_refs)):
        pl.when(pl.program_id(0) == i)(functools.partial(finish, mask, y_ref))


def project(acts, outs, p_in, p_out, masks, m, mib):
    examples = acts.shape[0] // SEQ
    rows = m * SEQ
    first = masks[0]

    def start(i):
        return first_example(lax.bitwise_xor(lax.axis_index("tensor"), first + i), m, examples) * SEQ

    shapes = [
        jax.ShapeDtypeStruct((rows + 16, LANES), jnp.bfloat16) if k else jax.ShapeDtypeStruct((rows, LANES), jnp.float32)
        for k in masks
    ]
    return pl.pallas_call(
        functools.partial(project_kernel, masks),
        grid=(len(masks),),
        in_specs=[
            pl.BlockSpec((pl.Element(rows), pl.Element(acts.shape[1])), lambda i: (start(i), 0)),
            pl.BlockSpec((pl.Element(rows), pl.Element(outs.shape[1])), lambda i: (start(i), 0)),
            pl.BlockSpec(p_in.shape, lambda i: (0, 0)),
            pl.BlockSpec(p_out.shape, lambda i: (0, 0)),
        ],
        out_specs=[pl.BlockSpec(s.shape, lambda i: (0, 0)) for s in shapes],
        scratch_shapes=[pltpu.VMEM((rows, LANES), jnp.float32)],
        out_shape=shapes,
        compiler_params=params(mib),
        cost_estimate=pl.CostEstimate(flops=1, bytes_accessed=1, transcendentals=0),
    )(acts, outs, p_in, p_out)


def split(v):
    hi = v.astype(jnp.bfloat16)
    return hi, (v - hi.astype(jnp.float32)).astype(jnp.bfloat16)


def grads_kernel(n, m, own, *refs):
    coded, out, z, block = refs[: n - 1], *refs[-3:]
    rows = m * SEQ
    x = own[...]
    for ref in coded:
        y = ref[...].astype(jnp.float32)
        x = x + root(y[:rows]) * y[rows : rows + 1]
    half = R // n // 2
    contract = (((1,), (0,)), ((), ()))
    for e in range(m):
        xe = x[e * SEQ : (e + 1) * SEQ, :]
        hi, lo = split(xe)
        hi_t, lo_t = split(xe.T)
        first = lax.dot_general(jnp.concatenate([hi_t, lo_t], 0), hi, contract, preferred_element_type=jnp.float32)
        last = lax.dot_general(hi_t, lo, contract, preferred_element_type=jnp.float32)
        z[e] = first[:LANES] + first[LANES:] + last
    for j in range(n):
        for e in range(m):
            even = z[e, pl.ds(2 * half * j, half, stride=2), :]
            odd = z[e, pl.ds(2 * half * j + 1, half, stride=2), :]
            g = jnp.concatenate([even[:, R:], odd[:, R:]], 1)
            top = column_top(g)
            block[pl.ds(e, half, stride=m), :] = power(g, top)
            block[pl.ds(half * m + e, 1), :] = top
        y = block[...].astype(jnp.bfloat16)
        for t in range(n):
            out[j * n + t] = y


def grads_of(own, coded, wait_for, n, m):
    rows = (R // n // 2 + 1) * m
    return pl.pallas_call(
        functools.partial(grads_kernel, n, m),
        in_specs=[pl.BlockSpec(memory_space=pltpu.VMEM)] * n + [pl.BlockSpec(memory_space=pl.ANY)] * len(wait_for),
        out_specs=pl.BlockSpec(memory_space=pltpu.VMEM),
        out_shape=jax.ShapeDtypeStruct((n * n, rows, LANES), jnp.bfloat16),
        scratch_shapes=[pltpu.VMEM((m, SEQ, LANES), jnp.float32), pltpu.VMEM((rows, LANES), jnp.float32)],
        compiler_params=params(24),
        cost_estimate=pl.CostEstimate(flops=1, bytes_accessed=1, transcendentals=0),
    )(own, *coded, *wait_for)


def scores_kernel(n, m, examples, masks, h, *refs):
    grads, queries, out, a = refs[0], refs[1 : n + 1], refs[n + 1], refs[n + 2]
    half = R // n // 2
    rows = n * n * m
    for s in range(n * n):
        y = grads[s].astype(jnp.float32)
        top = y[half * m :]
        w = root(y[: half * m]) * (1.0 / TOP)
        for r in range(half):
            a[pl.ds(s * m, m), pl.ds(r * LANES, LANES)] = w[r * m : (r + 1) * m] * top
    contract = (((1,), (0,)), ((), ()))
    hi, lo = split(a[...])
    left = jnp.concatenate([hi, lo], 0)
    step = min(256, h.shape[0])
    top, low = None, None
    for k in range(0, h.shape[0], step):
        h_hi, h_lo = split(h[pl.ds(k, step), :])
        one = lax.dot_general(left[:, k : k + step], h_hi, contract, preferred_element_type=jnp.float32)
        two = lax.dot_general(hi[:, k : k + step], h_lo, contract, preferred_element_type=jnp.float32)
        top, low = (one, two) if top is None else (top + one, low + two)
    hi, lo = split(top[:rows] + top[rows:] + low)
    both = jnp.concatenate([hi, lo], 0)
    d = lax.axis_index("dp")
    for mask, ref in zip(masks, queries):
        to = lax.bitwise_xor(d, mask)
        s = lax.dot_general(both, ref[...], ROWS_CONTRACT, preferred_element_type=jnp.float32)
        s = s[:rows] + s[rows:]
        for p in range(n):
            kept, done = [], 0
            while done < examples:
                owner = min(done // m, n - 1)
                begin = min(owner * m, examples - m)
                at = (p * n + owner) * m
                kept.append(s[at + done - begin : at + m])
                done = begin + m
            part = jnp.concatenate(kept, 0)
            top = column_top(part)
            out[p * n + to] = jnp.concatenate([power(part, top), top], 0).astype(jnp.bfloat16)


def scores_of(h, queries, grads, n, m, examples):
    masks = sorted(queries)
    blocks = [queries[k] for k in masks]
    width = blocks[0].shape[0]
    return pl.pallas_call(
        functools.partial(scores_kernel, n, m, examples, masks),
        in_specs=[pl.BlockSpec(memory_space=pltpu.VMEM)] * (2 + n),
        out_specs=pl.BlockSpec(memory_space=pltpu.VMEM),
        out_shape=jax.ShapeDtypeStruct((n * n, examples + 1, width), jnp.bfloat16),
        scratch_shapes=[pltpu.VMEM((n * n * m, R // n // 2 * LANES), jnp.float32)],
        compiler_params=params(40),
    )(h, grads, *blocks)


def unpack_kernel(examples, scale, y_ref, out):
    def term(i):
        y = y_ref[i].astype(jnp.float32)
        return root(y[:examples]) * y[examples:]

    count = y_ref.shape[0]
    if count <= 16:
        total = sum(term(i) for i in range(count))
    else:
        total = lax.fori_loop(1, count, lambda i, c: c + term(i), term(0))
    out[...] = total * scale


def unpack(y, scale):
    examples = y.shape[1] - 1
    return pl.pallas_call(
        functools.partial(unpack_kernel, examples, scale),
        in_specs=[pl.BlockSpec(memory_space=pltpu.VMEM)],
        out_specs=pl.BlockSpec(memory_space=pltpu.VMEM),
        out_shape=jax.ShapeDtypeStruct((examples, y.shape[2]), jnp.float32),
        compiler_params=params(24),
    )(y)


def local(n, activations, out_grads, proj_in, proj_out, hess_inv, queries):
    bits = n.bit_length() - 1
    examples = activations.shape[0] // SEQ
    m = -(-examples // n)
    def along(v, mask):
        return lax.ppermute(v, "tensor", [(i, i ^ mask) for i in range(n)])

    def flip(v, mask):
        return lax.ppermute(v, "dp", [(i, i ^ mask) for i in range(n)])

    def after(v, first):
        return lax.optimization_barrier((v, first))[0]

    all_q = {0: queries}
    all_q[n // 2] = flip(queries, n // 2)

    far = list(range(2, n))
    y = project(activations, out_grads, proj_in, proj_out, far, m, 59)
    (near,) = project(activations, after(out_grads, y), proj_in, proj_out, [1], m, 59)
    (own,) = project(activations, after(out_grads, near), proj_in, proj_out, [0], m, 57)
    coded = [along(v, mask) for v, mask in zip(y, far)] + [along(near, 1)]
    grads = grads_of(own * TOP, coded, [all_q[n // 2]], n, m)
    for b in reversed(range(bits - 1)):
        all_q = dict(zip(all_q, after(tuple(all_q.values()), grads)))
        all_q.update({k | (1 << b): flip(v, 1 << b) for k, v in all_q.items()})

    grads_all = lax.all_to_all(grads, ("dp", "tensor"), 0, 0, tiled=True)
    out = scores_of(hess_inv, all_q, grads_all, n, m, examples)
    out = lax.all_to_all(out, ("dp", "tensor"), 0, 0, tiled=True)
    return unpack(out, (1.0 / math.sqrt(SEQ)) * (1.0 / math.sqrt(R * R)) / (TOP * TOP) / TOP)


def solution(mesh):
    n = mesh.shape["tensor"]
    return jax.shard_map(
        functools.partial(local, n),
        mesh=mesh,
        in_specs=(
            P(("groups", "dp"), "tensor"),
            P(("groups", "dp"), "tensor"),
            P(None, "tensor"),
            P(None, "tensor"),
            P("dp", "tensor"),
            P("dp", "tensor"),
        ),
        out_specs=P(("groups", "dp"), "tensor"),
        check_vma=False,
    )
```
